512 devices in a mesh: ctx: 256 (over z, y, x), uly: 2 (over core).
Axes of the slice: x: 4, y: 8, z: 8, core: 2. Of those that a mesh axis runs over, the one named last changes fastest.
Arguments:
- queries: bfloat16 [65536, 2048], P(('ctx', 'uly')), may hold values from -8 to 8
- keys: bfloat16 [65536, 512], P(('ctx', 'uly')), may hold values from -3 to 3
- values: bfloat16 [65536, 512], P(('ctx', 'uly')), may hold values from -6 to 6
- output_gradient: bfloat16 [65536, 2048], P(('ctx', 'uly')), may hold values from -6 to 6
- segment_ids: int32 [65536], replicated, may hold values from 0 to 255, never falling along the last dimension, each value on 1 to 513 neighbouring positions
Outputs:
- attn_out: bfloat16 [65536, 2048], P(('ctx', 'uly'))
- query_grad: bfloat16 [65536, 2048], P(('ctx', 'uly'))
- key_gradient: bfloat16 [65536, 512], P(('ctx', 'uly'))
- value_gradient: bfloat16 [65536, 512], P(('ctx', 'uly'))
The draws below stay inside these ranges and needn't reach their ends.
Inputs may be any that keep to these rules, and one draw needn't show every extreme that they name: `segment_ids`: segment numbers never fall along the window; each document holds 1 to 513 consecutive tokens, and one holds exactly 513.
All inputs are finite; a program needn't handle non-finite values.
Results may differ from the reference program's by a relative error of at most 0.03.
Values may be sent and summed in bfloat16 or wider, within the bound.
A program may use at most 64 MiB of HBM per device.

```python
import math
import jax
import jax.numpy as jnp
import numpy as np
from jax import lax

QUERY_HEADS = 16
KEY_VALUE_HEADS = 4
HEAD_SIZE = 128
REACH = 2
SHARD = 256
WINDOW_TOKENS = 65536
DOC_MOST = 513
DOCS = 256


def draw_queries(key, part):
    key = jax.random.fold_in(key, 11)
    final_result = jnp.clip(jax.random.normal(key, (WINDOW_TOKENS, QUERY_HEADS * HEAD_SIZE), jnp.float32), -3.0, 3.0)
    return final_result.astype(jnp.bfloat16)


def draw_keys(key, part):
    key = jax.random.fold_in(key, 23)
    final_result = jnp.clip(jax.random.normal(key, (WINDOW_TOKENS, KEY_VALUE_HEADS * HEAD_SIZE), jnp.float32), -3.0, 3.0)
    return final_result.astype(jnp.bfloat16)


def level_of(own_key, extent, cuts, least, largest):
    factor_of = 1.0
    for axis_at, blocks in cuts:
        draws = jax.random.uniform(jax.random.fold_in(jax.random.fold_in(own_key, 6), axis_at), (blocks,), jnp.float32, least / len(cuts), largest / len(cuts))
        factor_of = factor_of * jnp.repeat(jnp.exp(draws), extent[axis_at] // blocks).reshape((-1,) + (1,) * (len(extent) - 1 - axis_at))
    return factor_of


def profile(amount, total, reach, slope):
    weights = [(1 << 20) // math.isqrt(standing ** slope) + 1 for standing in range(2, amount + 1)]
    surplus, given = total - reach - (amount - 1), [1] * (amount - 1)
    while surplus > 0:
        candidates = [i for i in range(amount - 1) if given[i] < reach]
        pool, left = sum([weights[i] for i in candidates]), surplus
        for i in candidates:
            more = min(reach - given[i], max(1, left * weights[i] // pool), surplus)
            given[i] = given[i] + more
            surplus = surplus - more
    return np.array([reach] + given)


def uneven_parts(key, number_of, total, limit, skew):
    if number_of == 2:
        one = jax.random.randint(key, (), max(1, total - limit), min(limit, total - 1) + 1)
        return jnp.stack([one, total - one])
    sizes = jnp.asarray(profile(number_of, total, limit, skew), jnp.int32)
    couples = (number_of - 1) // 2
    donor, taker = sizes[1:1 + 2 * couples:2], sizes[2:2 + 2 * couples:2]
    slack = jnp.minimum(donor - 1, limit - taker)
    moved = jax.random.randint(jax.random.fold_in(key, 1), (couples,), 0, 1 << 20) % (slack + 1)
    sizes = sizes.at[1:1 + 2 * couples:2].set(donor - moved).at[2:2 + 2 * couples:2].set(taker + moved)
    return sizes[jax.random.permutation(jax.random.fold_in(key, 2), number_of)]


def scatter_about(key, shape, spread, limit, split=(), held_as=jnp.bfloat16):
    factor_of = level_of(key, shape, split, -0.22, 0.18) if split else 1.0
    result = jax.random.normal(key, shape, jnp.float32) * spread * factor_of
    return jnp.minimum(jnp.maximum(result, -limit), limit).astype(held_as)


def setup_inputs(seed: int = 0) -> dict:
    key_of = jax.random.split(jax.random.key(seed), 6)
    queries = draw_queries(jax.random.fold_in(key_of[5], 71), 0)
    keys = draw_keys(jax.random.fold_in(key_of[5], 71), 0)
    values = scatter_about(key_of[2], (WINDOW_TOKENS, KEY_VALUE_HEADS * HEAD_SIZE), 1.0, 6.0, ((0, 512),))
    output_gradient = scatter_about(key_of[3], (WINDOW_TOKENS, QUERY_HEADS * HEAD_SIZE), 1.0, 6.0, ((0, 512),))
    segment_ids = jnp.searchsorted(jnp.cumsum(uneven_parts(key_of[4], DOCS, WINDOW_TOKENS, DOC_MOST, 2)), jnp.arange(WINDOW_TOKENS), side="right").astype(jnp.int32)
    return {"queries": queries, "keys": keys, "values": values, "output_gradient": output_gradient, "segment_ids": segment_ids}


def reference(queries, keys, values, output_gradient, segment_ids):
    group_width = QUERY_HEADS // KEY_VALUE_HEADS
    scaling = HEAD_SIZE ** -0.5
    window = (REACH + 1) * SHARD
    blocks = WINDOW_TOKENS // SHARD
    leading_rows = REACH * SHARD
    query_collected = queries.reshape(WINDOW_TOKENS, KEY_VALUE_HEADS, group_width, HEAD_SIZE)
    gradient_collected = output_gradient.reshape(WINDOW_TOKENS, KEY_VALUE_HEADS, group_width, HEAD_SIZE)
    leading_part = jnp.zeros((leading_rows, KEY_VALUE_HEADS, HEAD_SIZE), jnp.bfloat16)
    key_padding = jnp.concatenate([leading_part, keys.reshape(WINDOW_TOKENS, KEY_VALUE_HEADS, HEAD_SIZE)], axis=0)
    value_padding = jnp.concatenate([leading_part, values.reshape(WINDOW_TOKENS, KEY_VALUE_HEADS, HEAD_SIZE)], axis=0)
    id_pad = jnp.concatenate([jnp.full((leading_rows,), -1, jnp.int32), segment_ids.astype(jnp.int32)])
    offsets = jnp.arange(window, dtype=jnp.int32)
    row_index = jnp.arange(SHARD, dtype=jnp.int32)

    def pieces(block):
        start = (block * SHARD).astype(jnp.int32)
        query_block = lax.dynamic_slice_in_dim(query_collected, start, SHARD)
        grad_block = lax.dynamic_slice_in_dim(gradient_collected, start, SHARD)
        key_block = lax.dynamic_slice_in_dim(key_padding, start, window)
        value_block = lax.dynamic_slice_in_dim(value_padding, start, window)
        query_ids = lax.dynamic_slice_in_dim(id_pad, start + leading_rows, SHARD)
        key_ids = lax.dynamic_slice_in_dim(id_pad, start, window)
        allowed = (query_ids[:, None] == key_ids[None, :]) & (offsets[None, :] <= row_index[:, None] + leading_rows)
        scores = jnp.einsum("qhgd,khd->hgqk", query_block.astype(jnp.float32), key_block.astype(jnp.float32)) * scaling
        return start, query_block, grad_block, key_block, value_block, allowed[None, None], scores

    def forward(block):
        start, query_block, grad_block, key_block, value_block, allowed, scores = pieces(block)
        highest = jnp.max(jnp.where(allowed, scores, -1e30), axis=-1)
        total = jnp.sum(jnp.where(allowed, jnp.exp(scores - highest[..., None]), 0.0), axis=-1)
        logsum = highest + jnp.log(total)
        probs = jnp.where(allowed, jnp.exp(scores - logsum[..., None]), 0.0)
        rounded = lax.optimization_barrier(probs.astype(jnp.bfloat16)).astype(jnp.float32)
        output = jnp.einsum("hgqk,khd->qhgd", rounded, value_block.astype(jnp.float32))
        return output.astype(jnp.bfloat16), logsum

    block_list = jnp.arange(blocks, dtype=jnp.int32)
    output_list, logsums = lax.map(forward, block_list)
    output_list = output_list.reshape(WINDOW_TOKENS, KEY_VALUE_HEADS, group_width, HEAD_SIZE)
    attn_out = output_list.reshape(WINDOW_TOKENS, QUERY_HEADS * HEAD_SIZE)
    delta = jnp.sum(gradient_collected.astype(jnp.float32) * output_list.astype(jnp.float32), axis=-1)

    def backward(carry, block):
        key_running_sum, value_running_sum = carry
        start, query_block, grad_block, key_block, value_block, allowed, scores = pieces(block)
        logsum = logsums[block]
        delta_block = jnp.transpose(lax.dynamic_slice_in_dim(delta, start, SHARD), (1, 2, 0))
        probs = jnp.where(allowed, jnp.exp(scores - logsum[..., None]), 0.0)
        rounded = lax.optimization_barrier(probs.astype(jnp.bfloat16)).astype(jnp.float32)
        grad_float = grad_block.astype(jnp.float32)
        value_part = jnp.einsum("hgqk,qhgd->khd", rounded, grad_float)
        dprob = jnp.einsum("qhgd,khd->hgqk", grad_float, value_block.astype(jnp.float32))
        dscore = probs * (dprob - delta_block[..., None])
        dscore = lax.optimization_barrier(dscore.astype(jnp.bfloat16)).astype(jnp.float32)
        query_part = jnp.einsum("hgqk,khd->qhgd", dscore, key_block.astype(jnp.float32)) * scaling
        key_part = jnp.einsum("hgqk,qhgd->khd", dscore, query_block.astype(jnp.float32)) * scaling
        key_running_sum = lax.dynamic_update_slice_in_dim(key_running_sum, lax.dynamic_slice_in_dim(key_running_sum, start, window) + key_part, start, 0)
        value_running_sum = lax.dynamic_update_slice_in_dim(value_running_sum, lax.dynamic_slice_in_dim(value_running_sum, start, window) + value_part, start, 0)
        return (key_running_sum, value_running_sum), query_part.astype(jnp.bfloat16)

    blank_buffer = jnp.zeros((leading_rows + WINDOW_TOKENS, KEY_VALUE_HEADS, HEAD_SIZE), jnp.float32)
    (key_running_sum, value_running_sum), query_parts = lax.scan(backward, (blank_buffer, blank_buffer), block_list)
    query_grad = query_parts.reshape(WINDOW_TOKENS, QUERY_HEADS * HEAD_SIZE)
    key_gradient = key_running_sum[leading_rows:].astype(jnp.bfloat16).reshape(WINDOW_TOKENS, KEY_VALUE_HEADS * HEAD_SIZE)
    value_gradient = value_running_sum[leading_rows:].astype(jnp.bfloat16).reshape(WINDOW_TOKENS, KEY_VALUE_HEADS * HEAD_SIZE)
    return (attn_out, query_grad, key_gradient, value_gradient)
```

```python
import functools
import math

import jax
import jax.numpy as jnp
from jax import lax
from jax.experimental import pallas as pl
from jax.experimental.pallas import tpu as pltpu
from jax.sharding import PartitionSpec as P

MESH = pl.DeviceIdType.MESH
HEAD = 128
BLOCK = 128
GROUP = 4
GROUP_WIDTH = GROUP * HEAD
LOCAL = 2
HALF = LOCAL * GROUP_WIDTH
REACH = 2
SPAN = 5
ROWS = SPAN * BLOCK
SCALE = HEAD ** -0.5
TO_EXP2 = SCALE * math.log2(math.e)
NONE = -1e30

f32 = jnp.float32
bf16 = jnp.bfloat16


def dot(a, b, ca, cb):
    return lax.dot_general(a, b, (((ca,), (cb,)), ((), ())), preferred_element_type=f32)


def kernel(chips, q_hbm, k_hbm, v_hbm, g_hbm, ids_hbm, o_hbm, dq_hbm, dk_ref, dv_ref,
           q_buf, g_buf, kv_buf, ids_buf, bias, acc, out_buf, part, got, grad_buf,
           own_sem, ids_sem, qs_send, qs_recv, kv_send, kv_recv, out_sem, out_recv, part_send, part_recv):
    c, u = lax.axis_index("ctx"), lax.axis_index("uly")
    other = 1 - u
    kv_hbm = (k_hbm, v_hbm)

    barrier = pltpu.get_barrier_semaphore()
    pl.semaphore_signal(barrier, inc=1, device_id=(c, other), device_id_type=MESH)
    for step in (1, 2):
        for t in (0, 1):
            @pl.when(c >= step)
            def _():
                pl.semaphore_signal(barrier, inc=1, device_id=(c - step, t), device_id_type=MESH)

            @pl.when(c + step < chips)
            def _():
                pl.semaphore_signal(barrier, inc=1, device_id=(c + step, t), device_id_type=MESH)

    def own_of(g):
        columns = pl.ds(pl.multiple_of(u * HALF + g * GROUP_WIDTH, GROUP_WIDTH), GROUP_WIDTH)
        narrow = pl.ds(pl.multiple_of((u * LOCAL + g) * HEAD, HEAD), HEAD)
        wide = [pltpu.make_async_copy(a.at[:, columns], b.at[u, g], own_sem.at[g, i])
                for i, (a, b) in enumerate(((q_hbm, q_buf), (g_hbm, g_buf)))]
        return wide + [pltpu.make_async_copy(kv_hbm[i].at[:, narrow], kv_buf.at[i, g, 4 + u], own_sem.at[g, 2 + i])
                       for i in range(2)]

    ids_copies = []
    for b in range(6):
        row = jnp.maximum(2 * c - 4 + b, 0)
        ids_copies.append(pltpu.make_async_copy(ids_hbm.at[pl.ds(row, 1)], ids_buf.at[b, pl.ds(0, 1)], ids_sem.at[b]))
    for copy in own_of(0) + ids_copies + own_of(1):
        copy.start()

    for step in (1, 2):
        for i in range(2):
            @pl.when(c < step)
            def _():
                for g in range(LOCAL):
                    for t in (0, 1):
                        kv_buf[i, g, 2 * (REACH - step) + t] = jnp.zeros((BLOCK, HEAD), bf16)

    heard = 1
    for step in (1, 2):
        heard = heard + 2 * jnp.where(c >= step, 1, 0) + 2 * jnp.where(c + step < chips, 1, 0)
    pl.semaphore_wait(barrier, heard)

    def halo(i, g, step, t):
        columns = pl.ds((t * LOCAL + g) * HEAD, HEAD)
        return pltpu.make_async_remote_copy(
            kv_hbm[i].at[:, columns], kv_buf.at[i, g, 2 * (REACH - step) + u],
            kv_send.at[i, g, step, t], kv_recv.at[i, g, step, u], device_id=(c + step, t), device_id_type=MESH)

    def swap_kv(i, g):
        columns = pl.ds(pl.multiple_of((other * LOCAL + g) * HEAD, HEAD), HEAD)
        return pltpu.make_async_remote_copy(
            kv_hbm[i].at[:, columns], kv_buf.at[i, g, 4 + u],
            kv_send.at[i, g, 0, 0], kv_recv.at[i, g, 0, 0], device_id=(c, other), device_id_type=MESH)

    def swap_q(i, g):
        columns = pl.ds(pl.multiple_of(other * HALF + g * GROUP_WIDTH, GROUP_WIDTH), GROUP_WIDTH)
        return pltpu.make_async_remote_copy(
            (q_hbm, g_hbm)[i].at[:, columns], (q_buf, g_buf)[i].at[u, g],
            qs_send.at[i, g], qs_recv.at[i, g], device_id=(c, other), device_id_type=MESH)

    for g in range(LOCAL):
        for step in (2, 1):
            @pl.when(c + step < chips)
            def _():
                for i in range(2):
                    for t in (0, 1):
                        halo(i, g, step, t).start()
        for i in range(2):
            swap_kv(i, g).start()
            swap_q(i, g).start()

    for copy in ids_copies:
        copy.wait()
    below = lax.broadcasted_iota(jnp.int32, (BLOCK, BLOCK), 0) <= lax.broadcasted_iota(jnp.int32, (BLOCK, BLOCK), 1)
    for b in range(6):
        key_ids = jnp.transpose(jnp.broadcast_to(ids_buf[b, 0:1, :], (BLOCK, BLOCK)))
        if b < 4:
            key_ids = jnp.where(c >= REACH - b // 2, key_ids, -1)
        for s in (0, 1):
            if not s <= b < s + SPAN:
                continue
            allowed = key_ids == jnp.broadcast_to(ids_buf[4 + s, 0:1, :], (BLOCK, BLOCK))
            if b == 4 + s:
                allowed = allowed & below
            bias[s, b - s] = jnp.where(allowed, 0.0, NONE)

    def out_local(i, s, g):
        columns = pl.ds(pl.multiple_of(u * HALF + g * GROUP_WIDTH, GROUP_WIDTH), GROUP_WIDTH)
        return pltpu.make_async_copy(out_buf.at[i, s, g], (o_hbm, dq_hbm)[i].at[:, columns], out_sem.at[i, 0, g])

    def out_remote(i, s, g):
        columns = pl.ds(pl.multiple_of(u * HALF + g * GROUP_WIDTH, GROUP_WIDTH), GROUP_WIDTH)
        return pltpu.make_async_remote_copy(
            out_buf.at[i, s, g], (o_hbm, dq_hbm)[i].at[:, columns],
            out_sem.at[i, 1, g], out_recv.at[i, g], device_id=(c, other), device_id_type=MESH)

    def partial(i, g, step, t):
        return pltpu.make_async_remote_copy(
            part.at[i, g, 2 * (REACH - step) + t], got.at[i, g, step, u],
            part_send.at[i, g, step, t], part_recv.at[i, g, step, u], device_id=(c - step, t), device_id_type=MESH)

    def partial_chip(i, g):
        return pltpu.make_async_remote_copy(
            part.at[i, g, 4 + other], got.at[i, g, 0, u],
            part_send.at[i, g, 0, 0], part_recv.at[i, g, 0, 0], device_id=(c, other), device_id_type=MESH)

    def tile(g, s):
        keys = kv_buf[0, g, pl.ds(s, SPAN)].reshape(ROWS, HEAD)
        vals = kv_buf[1, g, pl.ds(s, SPAN)].reshape(ROWS, HEAD)
        keys_t, vals_t = jnp.transpose(keys), jnp.transpose(vals)
        add = bias[s].reshape(ROWS, BLOCK)
        add = jnp.concatenate([add, add], axis=1)
        dk = jnp.zeros((ROWS, HEAD), f32)
        dv = jnp.zeros((ROWS, HEAD), f32)
        for pair in range(GROUP // 2):
            heads = [slice((2 * pair + h) * HEAD, (2 * pair + h + 1) * HEAD) for h in (0, 1)]
            qs = jnp.concatenate([q_buf[s, g, :, h] for h in heads], axis=0)
            gs = jnp.concatenate([g_buf[s, g, :, h] for h in heads], axis=0)
            scores = dot(keys, qs, 1, 1) * TO_EXP2 + add
            highest = jnp.max(scores, axis=0, keepdims=True)
            probs = jnp.exp2(scores - highest)
            probs = probs * (1.0 / jnp.sum(probs, axis=0, keepdims=True))
            rounded = probs.astype(bf16)
            dprobs = dot(vals, gs, 1, 1)
            delta = jnp.sum(probs * dprobs, axis=0, keepdims=True)
            dscores = (probs * (dprobs - delta)).astype(bf16)
            dv = dv + dot(rounded, gs, 1, 0)
            dk = dk + dot(dscores, qs, 1, 0)
            out_t = dot(vals_t, rounded, 1, 0)
            dq_t = dot(keys_t, dscores, 1, 0) * SCALE
            for h in (0, 1):
                out_buf[0, s, g, :, heads[h]] = jnp.transpose(out_t[:, h * BLOCK:(h + 1) * BLOCK]).astype(bf16)
                out_buf[1, s, g, :, heads[h]] = jnp.transpose(dq_t[:, h * BLOCK:(h + 1) * BLOCK]).astype(bf16)
        acc[0, pl.ds(s, SPAN)] += dk.reshape(SPAN, BLOCK, HEAD) * SCALE
        acc[1, pl.ds(s, SPAN)] += dv.reshape(SPAN, BLOCK, HEAD)

    def head(g, carry):
        for copy in own_of(g):
            copy.wait()
        for i in range(2):
            swap_kv(i, g).wait_recv()
            swap_q(i, g).wait_recv()
        for step in (1, 2):
            @pl.when(c >= step)
            def _():
                for i in range(2):
                    for t in (0, 1):
                        arrived(i, g, step, t).wait_recv()
        acc[...] = jnp.zeros(acc.shape, f32)
        tile(g, other)
        for i in range(2):
            out_remote(i, other, g).start()
        tile(g, u)
        for i in range(2):
            part[i, g] = acc[i].astype(bf16)
        for step in (2, 1):
            @pl.when(c >= step)
            def _():
                for i in range(2):
                    for t in (0, 1):
                        partial(i, g, step, t).start()
        for i in range(2):
            partial_chip(i, g).start()
            grad_buf[i, g, u] = acc[i, 4 + u]
            out_local(i, u, g).start()
        return carry

    def arrived(i, g, step, t):
        return pltpu.make_async_remote_copy(
            kv_hbm[i].at[:, pl.ds(0, HEAD)], kv_buf.at[i, g, 2 * (REACH - step) + t],
            kv_send.at[i, g, step, t], kv_recv.at[i, g, step, t], device_id=(c, other), device_id_type=MESH)

    def later(i, g, step, t):
        return pltpu.make_async_remote_copy(
            part.at[i, g, 0], got.at[i, g, step, t], part_send.at[i, g, step, t],
            part_recv.at[i, g, step, t], device_id=(c, other), device_id_type=MESH)

    lax.fori_loop(0, LOCAL, head, 0)

    for g in range(LOCAL):
        for i in range(2):
            partial_chip(i, g).wait_recv()
            grad_buf[i, g, other] = got[i, g, 0, other].astype(f32)
        for step in (1, 2):
            @pl.when(c + step < chips)
            def _():
                for i in range(2):
                    for t in (0, 1):
                        later(i, g, step, t).wait_recv()
                        grad_buf[i, g, t] += got[i, g, step, t].astype(f32)
        for i in range(2):
            for t in (0, 1):
                (dk_ref, dv_ref)[i][:, (t * LOCAL + g) * HEAD:(t * LOCAL + g + 1) * HEAD] = grad_buf[i, g, t].astype(bf16)

    for g in range(LOCAL):
        for i in range(2):
            out_remote(i, other, g).wait()
            out_local(i, u, g).wait()
            swap_kv(i, g).wait_send()
            swap_q(i, g).wait_send()
            partial_chip(i, g).wait_send()
        for step in (1, 2):
            @pl.when(c + step < chips)
            def _():
                for i in range(2):
                    for t in (0, 1):
                        halo(i, g, step, t).wait_send()

            @pl.when(c >= step)
            def _():
                for i in range(2):
                    for t in (0, 1):
                        partial(i, g, step, t).wait_send()


def deliver(a0, a1, a2, a3, b0, b1, b2, b3, sem):
    copies = [pltpu.make_async_copy(a, b, sem.at[i]) for i, (a, b) in enumerate(zip((a0, a1, a2, a3), (b0, b1, b2, b3)))]
    for copy in copies:
        copy.start()
    for copy in copies:
        copy.wait()


def solution(mesh):
    chips = mesh.shape["ctx"]
    tokens = P(("ctx", "uly"), None)

    def per_device(queries, keys, values, output_gradient, segment_ids):
        rows = queries.shape[0]
        wide = jax.ShapeDtypeStruct((rows, 2 * HALF), bf16)
        narrow = jax.ShapeDtypeStruct((rows, 2 * LOCAL * HEAD), bf16)
        anywhere = pl.BlockSpec(memory_space=pltpu.HBM)
        vmem = pl.BlockSpec(memory_space=pltpu.VMEM)
        dma = pltpu.SemaphoreType.DMA
        held = pl.pallas_call(
            functools.partial(kernel, chips),
            out_shape=(wide, wide, narrow, narrow),
            in_specs=[anywhere] * 5,
            out_specs=(anywhere, anywhere, vmem, vmem),
            scratch_shapes=[
                pltpu.VMEM((2, LOCAL, BLOCK, GROUP_WIDTH), bf16),
                pltpu.VMEM((2, LOCAL, BLOCK, GROUP_WIDTH), bf16),
                pltpu.VMEM((2, LOCAL, 6, BLOCK, HEAD), bf16),
                pltpu.VMEM((6, 8, BLOCK), jnp.int32),
                pltpu.VMEM((2, SPAN, BLOCK, BLOCK), f32),
                pltpu.VMEM((2, 6, BLOCK, HEAD), f32),
                pltpu.VMEM((2, 2, LOCAL, BLOCK, GROUP_WIDTH), bf16),
                pltpu.VMEM((2, LOCAL, 6, BLOCK, HEAD), bf16),
                pltpu.VMEM((2, LOCAL, 3, 2, BLOCK, HEAD), bf16),
                pltpu.VMEM((2, LOCAL, 2, BLOCK, HEAD), f32),
                dma((LOCAL, 4)),
                dma((6,)),
                dma((2, LOCAL)),
                dma((2, LOCAL)),
                dma((2, LOCAL, 3, 2)),
                dma((2, LOCAL, 3, 2)),
                dma((2, 2, LOCAL)),
                dma((2, LOCAL)),
                dma((2, LOCAL, 3, 2)),
                dma((2, LOCAL, 3, 2)),
            ],
            compiler_params=pltpu.CompilerParams(
                collective_id=0, has_side_effects=True, vmem_limit_bytes=63 * 2 ** 20),
        )(queries, keys, values, output_gradient, segment_ids.reshape(-1, BLOCK))
        return pl.pallas_call(
            deliver, out_shape=(wide, wide, narrow, narrow), in_specs=[anywhere] * 4, out_specs=(anywhere,) * 4,
            scratch_shapes=[dma((4,))])(*held)

    return jax.shard_map(
        per_device, mesh=mesh, in_specs=(tokens,) * 4 + (P(),), out_specs=(tokens,) * 4, check_vma=False)
```

```python
import functools
import math

import jax
import jax.numpy as jnp
from jax import lax
from jax.experimental import pallas as pl
from jax.experimental.pallas import tpu as pltpu
from jax.sharding import PartitionSpec as P

MESH = pl.DeviceIdType.MESH
HEAD = 128
BLOCK = 128
GROUP = 4
GROUP_WIDTH = GROUP * HEAD
LOCAL = 2
HALF = LOCAL * GROUP_WIDTH
REACH = 2
SPAN = 5
ROWS = SPAN * BLOCK
SCALE = HEAD ** -0.5
TO_EXP2 = SCALE * math.log2(math.e)
NONE = -1e30

f32 = jnp.float32
bf16 = jnp.bfloat16


def dot(a, b, ca, cb):
    return lax.dot_general(a, b, (((ca,), (cb,)), ((), ())), preferred_element_type=f32)


def kernel(chips, q_hbm, k_hbm, v_hbm, g_hbm, ids_hbm, o_hbm, dq_hbm, dk_ref, dv_ref,
           q_buf, g_buf, kv_buf, ids_buf, bias, acc, out_buf, part, got, grad_buf, stage, probs_buf,
           own_sem, stage_sem, ids_sem, qs_send, qs_recv, kv_send, kv_recv, out_sem, out_recv, part_send, part_recv):
    c, u = lax.axis_index("ctx"), lax.axis_index("uly")
    other = 1 - u
    kv_hbm = (k_hbm, v_hbm)

    barrier = pltpu.get_barrier_semaphore()
    pl.semaphore_signal(barrier, inc=1, device_id=(c, other), device_id_type=MESH)
    for step in (1, 2):
        for t in (0, 1):
            @pl.when(c >= step)
            def _():
                pl.semaphore_signal(barrier, inc=1, device_id=(c - step, t), device_id_type=MESH)

            @pl.when(c + step < chips)
            def _():
                pl.semaphore_signal(barrier, inc=1, device_id=(c + step, t), device_id_type=MESH)

    def own_q(i, g):
        columns = pl.ds(pl.multiple_of(u * HALF + g * GROUP_WIDTH, GROUP_WIDTH), GROUP_WIDTH)
        return pltpu.make_async_copy((q_hbm, g_hbm)[i].at[:, columns], (q_buf, g_buf)[i].at[u, g], own_sem.at[g, i])

    def own_kv(i, g):
        narrow = pl.ds(pl.multiple_of((u * LOCAL + g) * HEAD, HEAD), HEAD)
        return pltpu.make_async_copy(kv_hbm[i].at[:, narrow], kv_buf.at[i, g, 4 + u], own_sem.at[g, 2 + i])

    def staged(i, g, t):
        return pltpu.make_async_copy(
            kv_hbm[i].at[:, pl.ds((t * LOCAL + g) * HEAD, HEAD)], stage.at[i, g, t], stage_sem.at[i, g, t])

    ids_copies = []
    for b in range(6):
        row = jnp.maximum(2 * c - 4 + b, 0)
        ids_copies.append(pltpu.make_async_copy(ids_hbm.at[pl.ds(row, 1)], ids_buf.at[b, pl.ds(0, 1)], ids_sem.at[b]))
    for g in range(LOCAL):
        for i in range(2):
            for t in (0, 1):
                staged(i, g, t).start()
    for copy in ids_copies:
        copy.start()
    for g in range(LOCAL):
        for i in range(2):
            own_kv(i, g).start()
            own_q(i, g).start()

    for step in (1, 2):
        for i in range(2):
            @pl.when(c < step)
            def _():
                for g in range(LOCAL):
                    for t in (0, 1):
                        kv_buf[i, g, 2 * (REACH - step) + t] = jnp.zeros((BLOCK, HEAD), bf16)

    heard = 1
    for step in (1, 2):
        heard = heard + 2 * jnp.where(c >= step, 1, 0) + 2 * jnp.where(c + step < chips, 1, 0)
    for g in range(LOCAL):
        for i in range(2):
            for t in (0, 1):
                staged(i, g, t).wait()
    pl.semaphore_wait(barrier, heard)

    def halo(i, g, step, t):
        return pltpu.make_async_remote_copy(
            stage.at[i, g, t], kv_buf.at[i, g, 2 * (REACH - step) + u],
            kv_send.at[i, g, step, t], kv_recv.at[i, g, step, u], device_id=(c + step, t), device_id_type=MESH)

    def swap_kv(i, g):
        return pltpu.make_async_remote_copy(
            stage.at[i, g, other], kv_buf.at[i, g, 4 + u],
            kv_send.at[i, g, 0, 0], kv_recv.at[i, g, 0, 0], device_id=(c, other), device_id_type=MESH)

    def swap_q(i, g):
        columns = pl.ds(pl.multiple_of(other * HALF + g * GROUP_WIDTH, GROUP_WIDTH), GROUP_WIDTH)
        return pltpu.make_async_remote_copy(
            (q_hbm, g_hbm)[i].at[:, columns], (q_buf, g_buf)[i].at[u, g],
            qs_send.at[i, g], qs_recv.at[i, g], device_id=(c, other), device_id_type=MESH)

    def send_halo(i, g):
        for step in (2, 1):
            @pl.when(c + step < chips)
            def _():
                for t in (0, 1):
                    halo(i, g, step, t).start()

    def halo_left(i, g):
        for step in (2, 1):
            @pl.when(c + step < chips)
            def _():
                for t in (0, 1):
                    halo(i, g, step, t).wait_send()

    def halo_here(i, g):
        for step in (1, 2):
            @pl.when(c >= step)
            def _():
                for t in (0, 1):
                    arrived(i, g, step, t).wait_recv()

    for i in range(2):
        send_halo(i, 0)
    for g in range(LOCAL):
        swap_kv(0, g).start()
        for i in range(2):
            swap_q(i, g).start()
        swap_kv(1, g).start()

    for copy in ids_copies:
        copy.wait()
    below = lax.broadcasted_iota(jnp.int32, (BLOCK, BLOCK), 0) <= lax.broadcasted_iota(jnp.int32, (BLOCK, BLOCK), 1)
    for b in range(6):
        key_ids = jnp.transpose(jnp.broadcast_to(ids_buf[b, 0:1, :], (BLOCK, BLOCK)))
        if b < 4:
            key_ids = jnp.where(c >= REACH - b // 2, key_ids, -1)
        for s in (0, 1):
            if not s <= b < s + SPAN:
                continue
            allowed = key_ids == jnp.broadcast_to(ids_buf[4 + s, 0:1, :], (BLOCK, BLOCK))
            if b == 4 + s:
                allowed = allowed & below
            bias[s, b - s] = jnp.where(allowed, 0.0, NONE)

    halo_left(0, 0)
    send_halo(0, 1)

    def out_local(i, s, g):
        columns = pl.ds(pl.multiple_of(u * HALF + g * GROUP_WIDTH, GROUP_WIDTH), GROUP_WIDTH)
        return pltpu.make_async_copy(out_buf.at[i, s, g], (o_hbm, dq_hbm)[i].at[:, columns], out_sem.at[i, 0, g])

    def out_remote(i, s, g):
        columns = pl.ds(pl.multiple_of(u * HALF + g * GROUP_WIDTH, GROUP_WIDTH), GROUP_WIDTH)
        return pltpu.make_async_remote_copy(
            out_buf.at[i, s, g], (o_hbm, dq_hbm)[i].at[:, columns],
            out_sem.at[i, 1, g], out_recv.at[i, g], device_id=(c, other), device_id_type=MESH)

    def partial(i, g, step, t):
        return pltpu.make_async_remote_copy(
            part.at[i, g, 2 * (REACH - step) + t], got.at[i, g, step, u],
            part_send.at[i, g, step, t], part_recv.at[i, g, step, u], device_id=(c - step, t), device_id_type=MESH)

    def partial_chip(i, g):
        return pltpu.make_async_remote_copy(
            part.at[i, g, 4 + other], got.at[i, g, 0, u],
            part_send.at[i, g, 0, 0], part_recv.at[i, g, 0, 0], device_id=(c, other), device_id_type=MESH)

    def pairs(g, s):
        for pair in range(GROUP // 2):
            heads = [slice((2 * pair + h) * HEAD, (2 * pair + h + 1) * HEAD) for h in (0, 1)]
            yield pair, heads, [jnp.concatenate([buf[s, g, :, h] for h in heads], axis=0) for buf in (q_buf, g_buf)]

    def first(g, s):
        keys = kv_buf[0, g, pl.ds(s, SPAN)].reshape(ROWS, HEAD)
        add = bias[s].reshape(ROWS, BLOCK)
        add = jnp.concatenate([add, add], axis=1)
        dv = jnp.zeros((ROWS, HEAD), f32)
        for pair, heads, (qs, gs) in pairs(g, s):
            scores = dot(keys, qs, 1, 1) * TO_EXP2 + add
            probs = jnp.exp2(scores - jnp.max(scores, axis=0, keepdims=True))
            probs = (probs * (1.0 / jnp.sum(probs, axis=0, keepdims=True))).astype(bf16)
            probs_buf[s, pair] = probs
            dv = dv + dot(probs, gs, 1, 0)
        acc[1, pl.ds(s, SPAN)] += dv.reshape(SPAN, BLOCK, HEAD)

    def second(g, s):
        keys = kv_buf[0, g, pl.ds(s, SPAN)].reshape(ROWS, HEAD)
        vals = kv_buf[1, g, pl.ds(s, SPAN)].reshape(ROWS, HEAD)
        keys_t, vals_t = jnp.transpose(keys), jnp.transpose(vals)
        dk = jnp.zeros((ROWS, HEAD), f32)
        for pair, heads, (qs, gs) in pairs(g, s):
            rounded = probs_buf[s, pair]
            probs = rounded.astype(f32)
            dprobs = dot(vals, gs, 1, 1)
            delta = jnp.sum(probs * dprobs, axis=0, keepdims=True)
            dscores = (probs * (dprobs - delta)).astype(bf16)
            dk = dk + dot(dscores, qs, 1, 0)
            out_t = dot(vals_t, rounded, 1, 0)
            dq_t = dot(keys_t, dscores, 1, 0) * SCALE
            for h in (0, 1):
                out_buf[0, s, g, :, heads[h]] = jnp.transpose(out_t[:, h * BLOCK:(h + 1) * BLOCK]).astype(bf16)
                out_buf[1, s, g, :, heads[h]] = jnp.transpose(dq_t[:, h * BLOCK:(h + 1) * BLOCK]).astype(bf16)
        acc[0, pl.ds(s, SPAN)] += dk.reshape(SPAN, BLOCK, HEAD) * SCALE

    def send_partials(i, g):
        part[i, g] = acc[i].astype(bf16)
        for step in (2, 1):
            @pl.when(c >= step)
            def _():
                for t in (0, 1):
                    partial(i, g, step, t).start()
        partial_chip(i, g).start()
        grad_buf[i, g, u] = acc[i, 4 + u]

    def head(g, carry):
        for i in range(2):
            own_q(i, g).wait()
            own_kv(i, g).wait()
        swap_kv(0, g).wait_recv()
        for i in range(2):
            swap_q(i, g).wait_recv()
        acc[...] = jnp.zeros(acc.shape, f32)
        halo_here(0, g)
        first(g, other)
        first(g, u)
        send_partials(1, g)

        @pl.when(g == 0)
        def _():
            halo_left(1, 0)
            send_halo(1, 1)

        swap_kv(1, g).wait_recv()
        halo_here(1, g)
        second(g, other)
        for i in range(2):
            out_remote(i, other, g).start()
        second(g, u)
        send_partials(0, g)
        for i in range(2):
            out_local(i, u, g).start()
        return carry

    def arrived(i, g, step, t):
        return pltpu.make_async_remote_copy(
            stage.at[i, g, 0], kv_buf.at[i, g, 2 * (REACH - step) + t],
            kv_send.at[i, g, step, t], kv_recv.at[i, g, step, t], device_id=(c, other), device_id_type=MESH)

    def later(i, g, step, t):
        return pltpu.make_async_remote_copy(
            part.at[i, g, 0], got.at[i, g, step, t], part_send.at[i, g, step, t],
            part_recv.at[i, g, step, t], device_id=(c, other), device_id_type=MESH)

    lax.fori_loop(0, LOCAL, head, 0)

    for g in range(LOCAL):
        for i in (1, 0):
            partial_chip(i, g).wait_recv()
            grad_buf[i, g, other] = got[i, g, 0, other].astype(f32)
            for step in (1, 2):
                @pl.when(c + step < chips)
                def _():
                    for t in (0, 1):
                        later(i, g, step, t).wait_recv()
                        grad_buf[i, g, t] += got[i, g, step, t].astype(f32)
            for t in (0, 1):
                (dk_ref, dv_ref)[i][:, (t * LOCAL + g) * HEAD:(t * LOCAL + g + 1) * HEAD] = grad_buf[i, g, t].astype(bf16)

    for i in range(2):
        halo_left(i, 1)
    for g in range(LOCAL):
        for i in range(2):
            out_remote(i, other, g).wait()
            out_local(i, u, g).wait()
            swap_kv(i, g).wait_send()
            swap_q(i, g).wait_send()
            partial_chip(i, g).wait_send()
        for step in (1, 2):
            @pl.when(c >= step)
            def _():
                for i in range(2):
                    for t in (0, 1):
                        partial(i, g, step, t).wait_send()


def deliver(a0, a1, a2, a3, b0, b1, b2, b3, sem):
    copies = [pltpu.make_async_copy(a, b, sem.at[i]) for i, (a, b) in enumerate(zip((a0, a1, a2, a3), (b0, b1, b2, b3)))]
    for copy in copies:
        copy.start()
    for copy in copies:
        copy.wait()


def solution(mesh):
    chips = mesh.shape["ctx"]
    tokens = P(("ctx", "uly"), None)

    def per_device(queries, keys, values, output_gradient, segment_ids):
        rows = queries.shape[0]
        wide = jax.ShapeDtypeStruct((rows, 2 * HALF), bf16)
        narrow = jax.ShapeDtypeStruct((rows, 2 * LOCAL * HEAD), bf16)
        anywhere = pl.BlockSpec(memory_space=pltpu.HBM)
        vmem = pl.BlockSpec(memory_space=pltpu.VMEM)
        dma = pltpu.SemaphoreType.DMA
        held = pl.pallas_call(
            functools.partial(kernel, chips),
            out_shape=tuple(pltpu.VMEM(x.shape, x.dtype) for x in (wide, wide, narrow, narrow)),
            in_specs=[anywhere] * 5,
            out_specs=(vmem,) * 4,
            scratch_shapes=[
                pltpu.VMEM((2, LOCAL, BLOCK, GROUP_WIDTH), bf16),
                pltpu.VMEM((2, LOCAL, BLOCK, GROUP_WIDTH), bf16),
                pltpu.VMEM((2, LOCAL, 6, BLOCK, HEAD), bf16),
                pltpu.VMEM((6, 8, BLOCK), jnp.int32),
                pltpu.VMEM((2, SPAN, BLOCK, BLOCK), f32),
                pltpu.VMEM((2, 6, BLOCK, HEAD), f32),
                pltpu.VMEM((2, 2, LOCAL, BLOCK, GROUP_WIDTH), bf16),
                pltpu.VMEM((2, LOCAL, 6, BLOCK, HEAD), bf16),
                pltpu.VMEM((2, LOCAL, 3, 2, BLOCK, HEAD), bf16),
                pltpu.VMEM((2, LOCAL, 2, BLOCK, HEAD), f32),
                pltpu.VMEM((2, LOCAL, 2, BLOCK, HEAD), bf16),
                pltpu.VMEM((2, GROUP // 2, ROWS, 2 * BLOCK), bf16),
                dma((LOCAL, 4)),
                dma((2, LOCAL, 2)),
                dma((6,)),
                dma((2, LOCAL)),
                dma((2, LOCAL)),
                dma((2, LOCAL, 3, 2)),
                dma((2, LOCAL, 3, 2)),
                dma((2, 2, LOCAL)),
                dma((2, LOCAL)),
                dma((2, LOCAL, 3, 2)),
                dma((2, LOCAL, 3, 2)),
            ],
            compiler_params=pltpu.CompilerParams(
                collective_id=0, has_side_effects=True, vmem_limit_bytes=48 * 2 ** 20),
        )(*[pltpu.with_memory_space_constraint(x, pltpu.HBM) for x in (
            queries, keys, values, output_gradient, segment_ids.reshape(-1, BLOCK))])
        return pl.pallas_call(
            deliver, out_shape=(wide, wide, narrow, narrow), in_specs=[vmem] * 4, out_specs=(anywhere,) * 4,
            scratch_shapes=[dma((4,))], compiler_params=pltpu.CompilerParams(vmem_limit_bytes=2 ** 20))(
                *[pltpu.with_memory_space_constraint(x, pltpu.VMEM) for x in held])

    return jax.shard_map(
        per_device, mesh=mesh, in_specs=(tokens,) * 4 + (P(),), out_specs=(tokens,) * 4, check_vma=False)
```

```python
import functools
import math

import jax
import jax.numpy as jnp
from jax import lax
from jax.experimental import pallas as pl
from jax.experimental.pallas import tpu as pltpu
from jax.sharding import PartitionSpec as P

MESH = pl.DeviceIdType.MESH
HEAD = 128
BLOCK = 128
GROUP = 4
GROUP_WIDTH = GROUP * HEAD
LOCAL = 2
HALF = LOCAL * GROUP_WIDTH
REACH = 2
SPAN = 5
ROWS = SPAN * BLOCK
SCALE = HEAD ** -0.5
TO_EXP2 = SCALE * math.log2(math.e)
NONE = -1e30

f32 = jnp.float32
bf16 = jnp.bfloat16


def dot(a, b, ca, cb):
    return lax.dot_general(a, b, (((ca,), (cb,)), ((), ())), preferred_element_type=f32)


def kernel(chips, q_hbm, k_hbm, v_hbm, g_hbm, ids_hbm, o_hbm, dq_hbm, dk_ref, dv_ref,
           q_buf, g_buf, kv_buf, ids_buf, bias, acc, out_buf, part, got, grad_buf, stage, probs_buf, dscores_buf,
           own_sem, stage_sem, ids_sem, qs_send, qs_recv, kv_send, kv_recv, out_sem, out_recv, part_send, part_recv):
    c, u = lax.axis_index("ctx"), lax.axis_index("uly")
    other = 1 - u
    kv_hbm = (k_hbm, v_hbm)

    barrier = pltpu.get_barrier_semaphore()
    pl.semaphore_signal(barrier, inc=1, device_id=(c, other), device_id_type=MESH)
    for step in (1, 2):
        for t in (0, 1):
            @pl.when(c >= step)
            def _():
                pl.semaphore_signal(barrier, inc=1, device_id=(c - step, t), device_id_type=MESH)

            @pl.when(c + step < chips)
            def _():
                pl.semaphore_signal(barrier, inc=1, device_id=(c + step, t), device_id_type=MESH)

    def own_q(i, g):
        columns = pl.ds(pl.multiple_of(u * HALF + g * GROUP_WIDTH, GROUP_WIDTH), GROUP_WIDTH)
        return pltpu.make_async_copy((q_hbm, g_hbm)[i].at[:, columns], (q_buf, g_buf)[i].at[u, g], own_sem.at[g, i])

    def own_kv(i, g):
        narrow = pl.ds(pl.multiple_of((u * LOCAL + g) * HEAD, HEAD), HEAD)
        return pltpu.make_async_copy(kv_hbm[i].at[:, narrow], kv_buf.at[i, g, 4 + u], own_sem.at[g, 2 + i])

    def staged(i, g, t):
        return pltpu.make_async_copy(
            kv_hbm[i].at[:, pl.ds((t * LOCAL + g) * HEAD, HEAD)], stage.at[i, g, t], stage_sem.at[i, g, t])

    ids_copies = []
    for b in range(6):
        row = jnp.maximum(2 * c - 4 + b, 0)
        ids_copies.append(pltpu.make_async_copy(ids_hbm.at[pl.ds(row, 1)], ids_buf.at[b, pl.ds(0, 1)], ids_sem.at[b]))
    for g in range(LOCAL):
        for i in range(2):
            for t in (0, 1):
                staged(i, g, t).start()
    for copy in ids_copies:
        copy.start()
    for g in range(LOCAL):
        for i in range(2):
            own_kv(i, g).start()
            own_q(i, g).start()

    for step in (1, 2):
        for i in range(2):
            @pl.when(c < step)
            def _():
                for g in range(LOCAL):
                    for t in (0, 1):
                        kv_buf[i, g, 2 * (REACH - step) + t] = jnp.zeros((BLOCK, HEAD), bf16)

    heard = 1
    for step in (1, 2):
        heard = heard + 2 * jnp.where(c >= step, 1, 0) + 2 * jnp.where(c + step < chips, 1, 0)
    for g in range(LOCAL):
        for i in range(2):
            for t in (0, 1):
                staged(i, g, t).wait()
    pl.semaphore_wait(barrier, heard)

    def halo(i, g, step, t):
        return pltpu.make_async_remote_copy(
            stage.at[i, g, t], kv_buf.at[i, g, 2 * (REACH - step) + u],
            kv_send.at[i, g, step, t], kv_recv.at[i, g, step, u], device_id=(c + step, t), device_id_type=MESH)

    def swap_kv(i, g):
        return pltpu.make_async_remote_copy(
            stage.at[i, g, other], kv_buf.at[i, g, 4 + u],
            kv_send.at[i, g, 0, 0], kv_recv.at[i, g, 0, 0], device_id=(c, other), device_id_type=MESH)

    def swap_q(i, g):
        columns = pl.ds(pl.multiple_of(other * HALF + g * GROUP_WIDTH, GROUP_WIDTH), GROUP_WIDTH)
        return pltpu.make_async_remote_copy(
            (q_hbm, g_hbm)[i].at[:, columns], (q_buf, g_buf)[i].at[u, g],
            qs_send.at[i, g], qs_recv.at[i, g], device_id=(c, other), device_id_type=MESH)

    def send_halo(i, g):
        for step in (1, 2):
            @pl.when(c + step < chips)
            def _():
                for t in (0, 1):
                    halo(i, g, step, t).start()

    def halo_left(i, g):
        for step in (2, 1):
            @pl.when(c + step < chips)
            def _():
                for t in (0, 1):
                    halo(i, g, step, t).wait_send()

    def halo_here(i, g):
        for step in (1, 2):
            @pl.when(c >= step)
            def _():
                for t in (0, 1):
                    arrived(i, g, step, t).wait_recv()

    for i in range(2):
        send_halo(i, 0)
    for g in range(LOCAL):
        swap_kv(0, g).start()
        for i in range(2):
            swap_q(i, g).start()
        swap_kv(1, g).start()

    for copy in ids_copies:
        copy.wait()
    below = lax.broadcasted_iota(jnp.int32, (BLOCK, BLOCK), 0) <= lax.broadcasted_iota(jnp.int32, (BLOCK, BLOCK), 1)
    for b in range(6):
        key_ids = jnp.transpose(jnp.broadcast_to(ids_buf[b, 0:1, :], (BLOCK, BLOCK)))
        if b < 4:
            key_ids = jnp.where(c >= REACH - b // 2, key_ids, -1)
        for s in (0, 1):
            if not s <= b < s + SPAN:
                continue
            allowed = key_ids == jnp.broadcast_to(ids_buf[4 + s, 0:1, :], (BLOCK, BLOCK))
            if b == 4 + s:
                allowed = allowed & below
            bias[s, b - s] = jnp.where(allowed, 0.0, NONE)

    halo_left(0, 0)
    send_halo(0, 1)

    def out_local(i, s, g):
        columns = pl.ds(pl.multiple_of(u * HALF + g * GROUP_WIDTH, GROUP_WIDTH), GROUP_WIDTH)
        return pltpu.make_async_copy(out_buf.at[i, s, g], (o_hbm, dq_hbm)[i].at[:, columns], out_sem.at[i, 0, g])

    def out_remote(i, s, g):
        columns = pl.ds(pl.multiple_of(u * HALF + g * GROUP_WIDTH, GROUP_WIDTH), GROUP_WIDTH)
        return pltpu.make_async_remote_copy(
            out_buf.at[i, s, g], (o_hbm, dq_hbm)[i].at[:, columns],
            out_sem.at[i, 1, g], out_recv.at[i, g], device_id=(c, other), device_id_type=MESH)

    def partial(i, g, step, t):
        return pltpu.make_async_remote_copy(
            part.at[i, g, 2 * (REACH - step) + t], got.at[i, g, step, u],
            part_send.at[i, g, step, t], part_recv.at[i, g, step, u], device_id=(c - step, t), device_id_type=MESH)

    def partial_chip(i, g):
        return pltpu.make_async_remote_copy(
            part.at[i, g, 4 + other], got.at[i, g, 0, u],
            part_send.at[i, g, 0, 0], part_recv.at[i, g, 0, 0], device_id=(c, other), device_id_type=MESH)

    def pairs(g, s):
        for pair in range(GROUP // 2):
            heads = [slice((2 * pair + h) * HEAD, (2 * pair + h + 1) * HEAD) for h in (0, 1)]
            yield pair, heads, [jnp.concatenate([buf[s, g, :, h] for h in heads], axis=0) for buf in (q_buf, g_buf)]

    def first(g, s):
        keys = kv_buf[0, g, pl.ds(s, SPAN)].reshape(ROWS, HEAD)
        add = bias[s].reshape(ROWS, BLOCK)
        add = jnp.concatenate([add, add], axis=1)
        dv = jnp.zeros((ROWS, HEAD), f32)
        for pair, heads, (qs, gs) in pairs(g, s):
            scores = dot(keys, qs, 1, 1) * TO_EXP2 + add
            probs = jnp.exp2(scores - jnp.max(scores, axis=0, keepdims=True))
            probs = (probs * (1.0 / jnp.sum(probs, axis=0, keepdims=True))).astype(bf16)
            probs_buf[g, s, pair] = probs
            dv = dv + dot(probs, gs, 1, 0)
        acc[1, pl.ds(s, SPAN)] += dv.reshape(SPAN, BLOCK, HEAD)

    def second(g, s):
        vals = kv_buf[1, g, pl.ds(s, SPAN)].reshape(ROWS, HEAD)
        dk = jnp.zeros((ROWS, HEAD), f32)
        for pair, heads, (qs, gs) in pairs(g, s):
            probs = probs_buf[g, s, pair].astype(f32)
            dprobs = dot(vals, gs, 1, 1)
            delta = jnp.sum(probs * dprobs, axis=0, keepdims=True)
            dscores = (probs * (dprobs - delta)).astype(bf16)
            dscores_buf[g, s, pair] = dscores
            dk = dk + dot(dscores, qs, 1, 0)
        acc[0, pl.ds(s, SPAN)] += dk.reshape(SPAN, BLOCK, HEAD) * SCALE

    def third(g, s):
        keys_t = jnp.transpose(kv_buf[0, g, pl.ds(s, SPAN)].reshape(ROWS, HEAD))
        vals_t = jnp.transpose(kv_buf[1, g, pl.ds(s, SPAN)].reshape(ROWS, HEAD))
        for pair in range(GROUP // 2):
            out_t = dot(vals_t, probs_buf[g, s, pair], 1, 0)
            dq_t = dot(keys_t, dscores_buf[g, s, pair], 1, 0) * SCALE
            for h in (0, 1):
                head = slice((2 * pair + h) * HEAD, (2 * pair + h + 1) * HEAD)
                out_buf[0, s, g, :, head] = jnp.transpose(out_t[:, h * BLOCK:(h + 1) * BLOCK]).astype(bf16)
                out_buf[1, s, g, :, head] = jnp.transpose(dq_t[:, h * BLOCK:(h + 1) * BLOCK]).astype(bf16)

    def send_partials(i, g):
        part[i, g] = acc[i].astype(bf16)
        for step in (2, 1):
            @pl.when(c >= step)
            def _():
                for t in (0, 1):
                    partial(i, g, step, t).start()
        partial_chip(i, g).start()
        grad_buf[i, g, u] = acc[i, 4 + u]

    def head(g, carry):
        for i in range(2):
            own_q(i, g).wait()
            own_kv(i, g).wait()
        swap_kv(0, g).wait_recv()
        for i in range(2):
            swap_q(i, g).wait_recv()
        acc[...] = jnp.zeros(acc.shape, f32)
        halo_here(0, g)
        first(g, other)
        first(g, u)
        send_partials(1, g)

        @pl.when(g == 0)
        def _():
            halo_left(1, 0)
            send_halo(1, 1)

        swap_kv(1, g).wait_recv()
        halo_here(1, g)
        second(g, other)
        second(g, u)
        send_partials(0, g)
        return carry

    def rest(g, carry):
        third(g, other)
        for i in range(2):
            out_remote(i, other, g).start()
        third(g, u)
        for i in range(2):
            out_local(i, u, g).start()
        return carry

    def arrived(i, g, step, t):
        return pltpu.make_async_remote_copy(
            stage.at[i, g, 0], kv_buf.at[i, g, 2 * (REACH - step) + t],
            kv_send.at[i, g, step, t], kv_recv.at[i, g, step, t], device_id=(c, other), device_id_type=MESH)

    def later(i, g, step, t):
        return pltpu.make_async_remote_copy(
            part.at[i, g, 0], got.at[i, g, step, t], part_send.at[i, g, step, t],
            part_recv.at[i, g, step, t], device_id=(c, other), device_id_type=MESH)

    lax.fori_loop(0, LOCAL, head, 0)
    lax.fori_loop(0, LOCAL, rest, 0)

    for g in range(LOCAL):
        for i in (1, 0):
            partial_chip(i, g).wait_recv()
            grad_buf[i, g, other] = got[i, g, 0, other].astype(f32)
            for step in (1, 2):
                @pl.when(c + step < chips)
                def _():
                    for t in (0, 1):
                        later(i, g, step, t).wait_recv()
                        grad_buf[i, g, t] += got[i, g, step, t].astype(f32)
            for t in (0, 1):
                (dk_ref, dv_ref)[i][:, (t * LOCAL + g) * HEAD:(t * LOCAL + g + 1) * HEAD] = grad_buf[i, g, t].astype(bf16)

    for i in range(2):
        halo_left(i, 1)
    for g in range(LOCAL):
        for i in range(2):
            out_remote(i, other, g).wait()
            out_local(i, u, g).wait()
            swap_kv(i, g).wait_send()
            swap_q(i, g).wait_send()
            partial_chip(i, g).wait_send()
        for step in (1, 2):
            @pl.when(c >= step)
            def _():
                for i in range(2):
                    for t in (0, 1):
                        partial(i, g, step, t).wait_send()


def deliver(a0, a1, a2, a3, b0, b1, b2, b3, sem):
    copies = [pltpu.make_async_copy(a, b, sem.at[i]) for i, (a, b) in enumerate(zip((a0, a1, a2, a3), (b0, b1, b2, b3)))]
    for copy in copies:
        copy.start()
    for copy in copies:
        copy.wait()


def solution(mesh):
    chips = mesh.shape["ctx"]
    tokens = P(("ctx", "uly"), None)

    def per_device(queries, keys, values, output_gradient, segment_ids):
        rows = queries.shape[0]
        wide = jax.ShapeDtypeStruct((rows, 2 * HALF), bf16)
        narrow = jax.ShapeDtypeStruct((rows, 2 * LOCAL * HEAD), bf16)
        anywhere = pl.BlockSpec(memory_space=pltpu.HBM)
        vmem = pl.BlockSpec(memory_space=pltpu.VMEM)
        dma = pltpu.SemaphoreType.DMA
        held = pl.pallas_call(
            functools.partial(kernel, chips),
            out_shape=tuple(pltpu.VMEM(x.shape, x.dtype) for x in (wide, wide, narrow, narrow)),
            in_specs=[anywhere] * 5,
            out_specs=(vmem,) * 4,
            scratch_shapes=[
                pltpu.VMEM((2, LOCAL, BLOCK, GROUP_WIDTH), bf16),
                pltpu.VMEM((2, LOCAL, BLOCK, GROUP_WIDTH), bf16),
                pltpu.VMEM((2, LOCAL, 6, BLOCK, HEAD), bf16),
                pltpu.VMEM((6, 8, BLOCK), jnp.int32),
                pltpu.VMEM((2, SPAN, BLOCK, BLOCK), f32),
                pltpu.VMEM((2, 6, BLOCK, HEAD), f32),
                pltpu.VMEM((2, 2, LOCAL, BLOCK, GROUP_WIDTH), bf16),
                pltpu.VMEM((2, LOCAL, 6, BLOCK, HEAD), bf16),
                pltpu.VMEM((2, LOCAL, 3, 2, BLOCK, HEAD), bf16),
                pltpu.VMEM((2, LOCAL, 2, BLOCK, HEAD), f32),
                pltpu.VMEM((2, LOCAL, 2, BLOCK, HEAD), bf16),
                pltpu.VMEM((LOCAL, 2, GROUP // 2, ROWS, 2 * BLOCK), bf16),
                pltpu.VMEM((LOCAL, 2, GROUP // 2, ROWS, 2 * BLOCK), bf16),
                dma((LOCAL, 4)),
                dma((2, LOCAL, 2)),
                dma((6,)),
                dma((2, LOCAL)),
                dma((2, LOCAL)),
                dma((2, LOCAL, 3, 2)),
                dma((2, LOCAL, 3, 2)),
                dma((2, 2, LOCAL)),
                dma((2, LOCAL)),
                dma((2, LOCAL, 3, 2)),
                dma((2, LOCAL, 3, 2)),
            ],
            compiler_params=pltpu.CompilerParams(
                collective_id=0, has_side_effects=True, vmem_limit_bytes=48 * 2 ** 20),
        )(*[pltpu.with_memory_space_constraint(x, pltpu.HBM) for x in (
            queries, keys, values, output_gradient, segment_ids.reshape(-1, BLOCK))])
        return pl.pallas_call(
            deliver, out_shape=(wide, wide, narrow, narrow), in_specs=[vmem] * 4, out_specs=(anywhere,) * 4,
            scratch_shapes=[dma((4,))], compiler_params=pltpu.CompilerParams(vmem_limit_bytes=2 ** 20))(
                *[pltpu.with_memory_space_constraint(x, pltpu.VMEM) for x in held])

    return jax.shard_map(
        per_device, mesh=mesh, in_specs=(tokens,) * 4 + (P(),), out_specs=(tokens,) * 4, check_vma=False)
```

```python
import functools
import math

import jax
import jax.numpy as jnp
from jax import lax
from jax.experimental import pallas as pl
from jax.experimental.pallas import tpu as pltpu
from jax.sharding import PartitionSpec as P

MESH = pl.DeviceIdType.MESH
HEAD = 128
BLOCK = 128
GROUP = 4
GROUP_WIDTH = GROUP * HEAD
LOCAL = 2
HALF = LOCAL * GROUP_WIDTH
REACH = 2
RING = 4
SPAN = 5
ROWS = SPAN * BLOCK
SCALE = HEAD ** -0.5
TO_EXP2 = SCALE * math.log2(math.e)
NONE = -1e30

f32 = jnp.float32
bf16 = jnp.bfloat16


def dot(a, b, ca, cb):
    return lax.dot_general(a, b, (((ca,), (cb,)), ((), ())), preferred_element_type=f32)


def kernel(chips, q_hbm, k_hbm, v_hbm, g_hbm, ids_hbm, o_hbm, dq_hbm, dk_ref, dv_ref,
           q_buf, g_buf, kv_buf, ids_buf, bias, acc, out_buf, part, got, grad_buf, stage, probs_buf, dscores_buf,
           own_sem, stage_sem, ids_sem, qs_send, qs_recv, kv_send, kv_recv, out_sem, out_recv, part_send, part_recv):
    c, u = lax.axis_index("ctx"), lax.axis_index("uly")
    other = 1 - u
    kv_hbm = (k_hbm, v_hbm)
    odd = lax.rem(c, 2) == 1
    first_x = lax.rem(c, RING) == 0

    barrier = pltpu.get_barrier_semaphore()
    pl.semaphore_signal(barrier, inc=1, device_id=(c, other), device_id_type=MESH)
    for step in (1, 2):
        for t in (0, 1):
            @pl.when(c >= step)
            def _():
                pl.semaphore_signal(barrier, inc=1, device_id=(c - step, t), device_id_type=MESH)

            @pl.when(c + step < chips)
            def _():
                pl.semaphore_signal(barrier, inc=1, device_id=(c + step, t), device_id_type=MESH)

    def own_q(i, g):
        columns = pl.ds(pl.multiple_of(u * HALF + g * GROUP_WIDTH, GROUP_WIDTH), GROUP_WIDTH)
        return pltpu.make_async_copy((q_hbm, g_hbm)[i].at[:, columns], (q_buf, g_buf)[i].at[u, g], own_sem.at[g, i])

    def own_kv(i, g):
        narrow = pl.ds(pl.multiple_of((u * LOCAL + g) * HEAD, HEAD), HEAD)
        return pltpu.make_async_copy(kv_hbm[i].at[:, narrow], kv_buf.at[i, g, 4 + u], own_sem.at[g, 2 + i])

    def staged(i, g, t):
        return pltpu.make_async_copy(
            kv_hbm[i].at[:, pl.ds((t * LOCAL + g) * HEAD, HEAD)], stage.at[i, g, t], stage_sem.at[i, g, t])

    ids_copies = []
    for b in range(6):
        row = jnp.maximum(2 * c - 4 + b, 0)
        ids_copies.append(pltpu.make_async_copy(ids_hbm.at[pl.ds(row, 1)], ids_buf.at[b, pl.ds(0, 1)], ids_sem.at[b]))
    for g in range(LOCAL):
        for i in range(2):
            for t in (0, 1):
                staged(i, g, t).start()
    for copy in ids_copies:
        copy.start()
    for g in range(LOCAL):
        for i in range(2):
            own_kv(i, g).start()
            own_q(i, g).start()

    for step in (1, 2):
        for i in range(2):
            @pl.when(c < step)
            def _():
                for g in range(LOCAL):
                    for t in (0, 1):
                        kv_buf[i, g, 2 * (REACH - step) + t] = jnp.zeros((BLOCK, HEAD), bf16)

    heard = 1
    for step in (1, 2):
        heard = heard + 2 * jnp.where(c >= step, 1, 0) + 2 * jnp.where(c + step < chips, 1, 0)
    for g in range(LOCAL):
        for i in range(2):
            for t in (0, 1):
                staged(i, g, t).wait()
    pl.semaphore_wait(barrier, heard)

    def halo(i, g, step, t):
        return pltpu.make_async_remote_copy(
            stage.at[i, g, t], kv_buf.at[i, g, 2 * (REACH - step) + u],
            kv_send.at[i, g, step, t], kv_recv.at[i, g, step, u], device_id=(c + step, t), device_id_type=MESH)

    def swap_kv(i, g):
        return pltpu.make_async_remote_copy(
            stage.at[i, g, other], kv_buf.at[i, g, 4 + u],
            kv_send.at[i, g, 0, 0], kv_recv.at[i, g, 0, 0], device_id=(c, other), device_id_type=MESH)

    def swap_q(i, g):
        columns = pl.ds(pl.multiple_of(other * HALF + g * GROUP_WIDTH, GROUP_WIDTH), GROUP_WIDTH)
        return pltpu.make_async_remote_copy(
            (q_hbm, g_hbm)[i].at[:, columns], (q_buf, g_buf)[i].at[u, g],
            qs_send.at[i, g], qs_recv.at[i, g], device_id=(c, other), device_id_type=MESH)

    def send_halo(i, g):
        def to(step, when):
            @pl.when(when & (c + step < chips))
            def _():
                for t in (0, 1):
                    halo(i, g, step, t).start()

        to(1, odd)
        to(2, c >= 0)
        to(1, ~odd)

    def halo_left(i, g):
        for step in (2, 1):
            @pl.when(c + step < chips)
            def _():
                for t in (0, 1):
                    halo(i, g, step, t).wait_send()

    def halo_here(i, g):
        for step in (1, 2):
            @pl.when(c >= step)
            def _():
                for t in (0, 1):
                    arrived(i, g, step, t).wait_recv()

    for g in range(LOCAL):
        for i in range(2):
            send_halo(i, g)
    for g in range(LOCAL):
        swap_kv(0, g).start()
        for i in range(2):
            swap_q(i, g).start()
        swap_kv(1, g).start()

    for copy in ids_copies:
        copy.wait()
    below = lax.broadcasted_iota(jnp.int32, (BLOCK, BLOCK), 0) <= lax.broadcasted_iota(jnp.int32, (BLOCK, BLOCK), 1)
    for b in range(6):
        key_ids = jnp.transpose(jnp.broadcast_to(ids_buf[b, 0:1, :], (BLOCK, BLOCK)))
        if b < 4:
            key_ids = jnp.where(c >= REACH - b // 2, key_ids, -1)
        for s in (0, 1):
            if not s <= b < s + SPAN:
                continue
            allowed = key_ids == jnp.broadcast_to(ids_buf[4 + s, 0:1, :], (BLOCK, BLOCK))
            if b == 4 + s:
                allowed = allowed & below
            bias[s, b - s] = jnp.where(allowed, 0.0, NONE)


    def out_local(i, s, g):
        columns = pl.ds(pl.multiple_of(u * HALF + g * GROUP_WIDTH, GROUP_WIDTH), GROUP_WIDTH)
        return pltpu.make_async_copy(out_buf.at[i, s, g], (o_hbm, dq_hbm)[i].at[:, columns], out_sem.at[i, 0, g])

    def out_remote(i, s, g):
        columns = pl.ds(pl.multiple_of(u * HALF + g * GROUP_WIDTH, GROUP_WIDTH), GROUP_WIDTH)
        return pltpu.make_async_remote_copy(
            out_buf.at[i, s, g], (o_hbm, dq_hbm)[i].at[:, columns],
            out_sem.at[i, 1, g], out_recv.at[i, g], device_id=(c, other), device_id_type=MESH)

    def partial(i, g, step, t):
        return pltpu.make_async_remote_copy(
            part.at[i, g, 2 * (REACH - step) + t], got.at[i, g, step, u],
            part_send.at[i, g, step, t], part_recv.at[i, g, step, u], device_id=(c - step, t), device_id_type=MESH)

    def partial_chip(i, g):
        return pltpu.make_async_remote_copy(
            part.at[i, g, 4 + other], got.at[i, g, 0, u],
            part_send.at[i, g, 0, 0], part_recv.at[i, g, 0, 0], device_id=(c, other), device_id_type=MESH)

    def pairs(g, s):
        for pair in range(GROUP // 2):
            heads = [slice((2 * pair + h) * HEAD, (2 * pair + h + 1) * HEAD) for h in (0, 1)]
            yield pair, heads, [jnp.concatenate([buf[s, g, :, h] for h in heads], axis=0) for buf in (q_buf, g_buf)]

    def first(g, s):
        keys = kv_buf[0, g, pl.ds(s, SPAN)].reshape(ROWS, HEAD)
        add = bias[s].reshape(ROWS, BLOCK)
        add = jnp.concatenate([add, add], axis=1)
        dv = jnp.zeros((ROWS, HEAD), f32)
        for pair, heads, (qs, gs) in pairs(g, s):
            scores = dot(keys, qs, 1, 1) * TO_EXP2 + add
            probs = jnp.exp2(scores - jnp.max(scores, axis=0, keepdims=True))
            probs = (probs * (1.0 / jnp.sum(probs, axis=0, keepdims=True))).astype(bf16)
            probs_buf[g, s, pair] = probs
            dv = dv + dot(probs, gs, 1, 0)
        acc[1, pl.ds(s, SPAN)] += dv.reshape(SPAN, BLOCK, HEAD)

    def second(g, s):
        vals = kv_buf[1, g, pl.ds(s, SPAN)].reshape(ROWS, HEAD)
        dk = jnp.zeros((ROWS, HEAD), f32)
        for pair, heads, (qs, gs) in pairs(g, s):
            probs = probs_buf[g, s, pair].astype(f32)
            dprobs = dot(vals, gs, 1, 1)
            delta = jnp.sum(probs * dprobs, axis=0, keepdims=True)
            dscores = (probs * (dprobs - delta)).astype(bf16)
            dscores_buf[g, s, pair] = dscores
            dk = dk + dot(dscores, qs, 1, 0)
        acc[0, pl.ds(s, SPAN)] += dk.reshape(SPAN, BLOCK, HEAD) * SCALE

    def third(g, s):
        keys_t = jnp.transpose(kv_buf[0, g, pl.ds(s, SPAN)].reshape(ROWS, HEAD))
        vals_t = jnp.transpose(kv_buf[1, g, pl.ds(s, SPAN)].reshape(ROWS, HEAD))
        for pair in range(GROUP // 2):
            out_t = dot(vals_t, probs_buf[g, s, pair], 1, 0)
            dq_t = dot(keys_t, dscores_buf[g, s, pair], 1, 0) * SCALE
            for h in (0, 1):
                head = slice((2 * pair + h) * HEAD, (2 * pair + h + 1) * HEAD)
                out_buf[0, s, g, :, head] = jnp.transpose(out_t[:, h * BLOCK:(h + 1) * BLOCK]).astype(bf16)
                out_buf[1, s, g, :, head] = jnp.transpose(dq_t[:, h * BLOCK:(h + 1) * BLOCK]).astype(bf16)

    def send_partials(i, g):
        part[i, g] = acc[i].astype(bf16)
        def to(step, when):
            @pl.when(when & (c >= step))
            def _():
                for t in (0, 1):
                    partial(i, g, step, t).start()

        to(1, first_x)
        to(2, c >= 0)
        to(1, ~first_x)
        partial_chip(i, g).start()
        grad_buf[i, g, u] = acc[i, 4 + u]

    def head(g, carry):
        for i in range(2):
            own_q(i, g).wait()
            own_kv(i, g).wait()
        swap_kv(0, g).wait_recv()
        for i in range(2):
            swap_q(i, g).wait_recv()
        acc[...] = jnp.zeros(acc.shape, f32)
        halo_here(0, g)
        first(g, other)
        first(g, u)
        send_partials(1, g)

        swap_kv(1, g).wait_recv()
        halo_here(1, g)
        second(g, other)
        second(g, u)
        send_partials(0, g)
        return carry

    def rest(g, carry):
        third(g, other)
        for i in range(2):
            out_remote(i, other, g).start()
        third(g, u)
        for i in range(2):
            out_local(i, u, g).start()
        return carry

    def arrived(i, g, step, t):
        return pltpu.make_async_remote_copy(
            stage.at[i, g, 0], kv_buf.at[i, g, 2 * (REACH - step) + t],
            kv_send.at[i, g, step, t], kv_recv.at[i, g, step, t], device_id=(c, other), device_id_type=MESH)

    def later(i, g, step, t):
        return pltpu.make_async_remote_copy(
            part.at[i, g, 0], got.at[i, g, step, t], part_send.at[i, g, step, t],
            part_recv.at[i, g, step, t], device_id=(c, other), device_id_type=MESH)

    lax.fori_loop(0, LOCAL, head, 0)
    lax.fori_loop(0, LOCAL, rest, 0)

    for g in range(LOCAL):
        for i in (1, 0):
            partial_chip(i, g).wait_recv()
            grad_buf[i, g, other] = got[i, g, 0, other].astype(f32)
            for step in (1, 2):
                @pl.when(c + step < chips)
                def _():
                    for t in (0, 1):
                        later(i, g, step, t).wait_recv()
                        grad_buf[i, g, t] += got[i, g, step, t].astype(f32)
            for t in (0, 1):
                (dk_ref, dv_ref)[i][:, (t * LOCAL + g) * HEAD:(t * LOCAL + g + 1) * HEAD] = grad_buf[i, g, t].astype(bf16)

    for i in range(2):
        for g in range(LOCAL):
            halo_left(i, g)
    for g in range(LOCAL):
        for i in range(2):
            out_remote(i, other, g).wait()
            out_local(i, u, g).wait()
            swap_kv(i, g).wait_send()
            swap_q(i, g).wait_send()
            partial_chip(i, g).wait_send()
        for step in (1, 2):
            @pl.when(c >= step)
            def _():
                for i in range(2):
                    for t in (0, 1):
                        partial(i, g, step, t).wait_send()


def deliver(a0, a1, a2, a3, b0, b1, b2, b3, sem):
    copies = [pltpu.make_async_copy(a, b, sem.at[i]) for i, (a, b) in enumerate(zip((a0, a1, a2, a3), (b0, b1, b2, b3)))]
    for copy in copies:
        copy.start()
    for copy in copies:
        copy.wait()


def solution(mesh):
    chips = mesh.shape["ctx"]
    tokens = P(("ctx", "uly"), None)

    def per_device(queries, keys, values, output_gradient, segment_ids):
        rows = queries.shape[0]
        wide = jax.ShapeDtypeStruct((rows, 2 * HALF), bf16)
        narrow = jax.ShapeDtypeStruct((rows, 2 * LOCAL * HEAD), bf16)
        anywhere = pl.BlockSpec(memory_space=pltpu.HBM)
        vmem = pl.BlockSpec(memory_space=pltpu.VMEM)
        dma = pltpu.SemaphoreType.DMA
        held = pl.pallas_call(
            functools.partial(kernel, chips),
            out_shape=tuple(pltpu.VMEM(x.shape, x.dtype) for x in (wide, wide, narrow, narrow)),
            in_specs=[anywhere] * 5,
            out_specs=(vmem,) * 4,
            scratch_shapes=[
                pltpu.VMEM((2, LOCAL, BLOCK, GROUP_WIDTH), bf16),
                pltpu.VMEM((2, LOCAL, BLOCK, GROUP_WIDTH), bf16),
                pltpu.VMEM((2, LOCAL, 6, BLOCK, HEAD), bf16),
                pltpu.VMEM((6, 8, BLOCK), jnp.int32),
                pltpu.VMEM((2, SPAN, BLOCK, BLOCK), f32),
                pltpu.VMEM((2, 6, BLOCK, HEAD), f32),
                pltpu.VMEM((2, 2, LOCAL, BLOCK, GROUP_WIDTH), bf16),
                pltpu.VMEM((2, LOCAL, 6, BLOCK, HEAD), bf16),
                pltpu.VMEM((2, LOCAL, 3, 2, BLOCK, HEAD), bf16),
                pltpu.VMEM((2, LOCAL, 2, BLOCK, HEAD), f32),
                pltpu.VMEM((2, LOCAL, 2, BLOCK, HEAD), bf16),
                pltpu.VMEM((LOCAL, 2, GROUP // 2, ROWS, 2 * BLOCK), bf16),
                pltpu.VMEM((LOCAL, 2, GROUP // 2, ROWS, 2 * BLOCK), bf16),
                dma((LOCAL, 4)),
                dma((2, LOCAL, 2)),
                dma((6,)),
                dma((2, LOCAL)),
                dma((2, LOCAL)),
                dma((2, LOCAL, 3, 2)),
                dma((2, LOCAL, 3, 2)),
                dma((2, 2, LOCAL)),
                dma((2, LOCAL)),
                dma((2, LOCAL, 3, 2)),
                dma((2, LOCAL, 3, 2)),
            ],
            compiler_params=pltpu.CompilerParams(
                collective_id=0, has_side_effects=True, vmem_limit_bytes=48 * 2 ** 20),
        )(*[pltpu.with_memory_space_constraint(x, pltpu.HBM) for x in (
            queries, keys, values, output_gradient, segment_ids.reshape(-1, BLOCK))])
        return pl.pallas_call(
            deliver, out_shape=(wide, wide, narrow, narrow), in_specs=[vmem] * 4, out_specs=(anywhere,) * 4,
            scratch_shapes=[dma((4,))], compiler_params=pltpu.CompilerParams(vmem_limit_bytes=2 ** 20))(
                *[pltpu.with_memory_space_constraint(x, pltpu.VMEM) for x in held])

    return jax.shard_map(
        per_device, mesh=mesh, in_specs=(tokens,) * 4 + (P(),), out_specs=(tokens,) * 4, check_vma=False)
```

```python
import functools
import math

import jax
import jax.numpy as jnp
from jax import lax
from jax.experimental import pallas as pl
from jax.experimental.pallas import tpu as pltpu
from jax.sharding import PartitionSpec as P

MESH = pl.DeviceIdType.MESH
HEAD = 128
BLOCK = 128
GROUP = 4
GROUP_WIDTH = GROUP * HEAD
LOCAL = 2
HALF = LOCAL * GROUP_WIDTH
REACH = 2
RING = 4
SPAN = 5
ROWS = SPAN * BLOCK
SCALE = HEAD ** -0.5
TO_EXP2 = SCALE * math.log2(math.e)
NONE = -1e30

f32 = jnp.float32
bf16 = jnp.bfloat16


def dot(a, b, ca, cb):
    return lax.dot_general(a, b, (((ca,), (cb,)), ((), ())), preferred_element_type=f32)


def kernel(chips, q_hbm, k_hbm, v_hbm, g_hbm, ids_hbm, o_hbm, dq_hbm, dk_ref, dv_ref,
           q_buf, g_buf, kv_buf, ids_buf, bias, acc, out_buf, part, got, grad_buf, stage, probs_buf, dscores_buf,
           own_sem, stage_sem, ids_sem, qs_send, qs_recv, kv_send, kv_recv, out_sem, out_recv, part_send, part_recv):
    c, u = lax.axis_index("ctx"), lax.axis_index("uly")
    other = 1 - u
    kv_hbm = (k_hbm, v_hbm)
    odd = lax.rem(c, 2) == 1
    first_x = lax.rem(c, RING) == 0

    barrier = pltpu.get_barrier_semaphore()
    pl.semaphore_signal(barrier, inc=1, device_id=(c, other), device_id_type=MESH)
    for step in (1, 2):
        for t in (0, 1):
            @pl.when(c >= step)
            def _():
                pl.semaphore_signal(barrier, inc=1, device_id=(c - step, t), device_id_type=MESH)

    def own_q(i, g):
        columns = pl.ds(pl.multiple_of(u * HALF + g * GROUP_WIDTH, GROUP_WIDTH), GROUP_WIDTH)
        return pltpu.make_async_copy((q_hbm, g_hbm)[i].at[:, columns], (q_buf, g_buf)[i].at[u, g], own_sem.at[g, i])

    def own_kv(i, g):
        narrow = pl.ds(pl.multiple_of((u * LOCAL + g) * HEAD, HEAD), HEAD)
        return pltpu.make_async_copy(kv_hbm[i].at[:, narrow], kv_buf.at[i, g, 4 + u], own_sem.at[g, 2 + i])

    def staged(i, g, t):
        return pltpu.make_async_copy(
            kv_hbm[i].at[:, pl.ds((t * LOCAL + g) * HEAD, HEAD)], stage.at[i, g, t], stage_sem.at[i, g, t])

    ids_copies = []
    for b in range(6):
        row = jnp.maximum(2 * c - 4 + b, 0)
        ids_copies.append(pltpu.make_async_copy(ids_hbm.at[pl.ds(row, 1)], ids_buf.at[b, pl.ds(0, 1)], ids_sem.at[b]))
    for g in range(LOCAL):
        for i in range(2):
            for t in (0, 1):
                staged(i, g, t).start()
    for copy in ids_copies:
        copy.start()
    for g in range(LOCAL):
        for i in range(2):
            own_kv(i, g).start()
            own_q(i, g).start()

    for step in (1, 2):
        for i in range(2):
            @pl.when(c < step)
            def _():
                for g in range(LOCAL):
                    for t in (0, 1):
                        kv_buf[i, g, 2 * (REACH - step) + t] = jnp.zeros((BLOCK, HEAD), bf16)

    heard = 1
    for step in (1, 2):
        heard = heard + 2 * jnp.where(c + step < chips, 1, 0)
    for g in range(LOCAL):
        for i in range(2):
            for t in (0, 1):
                staged(i, g, t).wait()
    pl.semaphore_wait(barrier, heard)

    def halo(i, g, step, t):
        return pltpu.make_async_remote_copy(
            stage.at[i, g, t], kv_buf.at[i, g, 2 * (REACH - step) + u],
            kv_send.at[i, g, step, t], kv_recv.at[i, g, step, u], device_id=(c + step, t), device_id_type=MESH)

    def swap_kv(i, g):
        return pltpu.make_async_remote_copy(
            stage.at[i, g, other], kv_buf.at[i, g, 4 + u],
            kv_send.at[i, g, 0, 0], kv_recv.at[i, g, 0, 0], device_id=(c, other), device_id_type=MESH)

    def swap_q(i, g):
        columns = pl.ds(pl.multiple_of(other * HALF + g * GROUP_WIDTH, GROUP_WIDTH), GROUP_WIDTH)
        return pltpu.make_async_remote_copy(
            (q_hbm, g_hbm)[i].at[:, columns], (q_buf, g_buf)[i].at[u, g],
            qs_send.at[i, g], qs_recv.at[i, g], device_id=(c, other), device_id_type=MESH)

    def send_halo(i, g):
        def to(step, when):
            @pl.when(when & (c + step < chips))
            def _():
                for t in (0, 1):
                    halo(i, g, step, t).start()

        to(1, odd)
        to(2, c >= 0)
        to(1, ~odd)

    def halo_left(i, g):
        for step in (2, 1):
            @pl.when(c + step < chips)
            def _():
                for t in (0, 1):
                    halo(i, g, step, t).wait_send()

    def halo_here(i, g):
        for step in (1, 2):
            @pl.when(c >= step)
            def _():
                for t in (0, 1):
                    arrived(i, g, step, t).wait_recv()

    for g in range(LOCAL):
        for i in range(2):
            send_halo(i, g)
    for g in range(LOCAL):
        swap_kv(0, g).start()
        for i in range(2):
            swap_q(i, g).start()
        swap_kv(1, g).start()

    for copy in ids_copies:
        copy.wait()
    below = lax.broadcasted_iota(jnp.int32, (BLOCK, BLOCK), 0) <= lax.broadcasted_iota(jnp.int32, (BLOCK, BLOCK), 1)
    for b in range(6):
        key_ids = jnp.transpose(jnp.broadcast_to(ids_buf[b, 0:1, :], (BLOCK, BLOCK)))
        if b < 4:
            key_ids = jnp.where(c >= REACH - b // 2, key_ids, -1)
        for s in (0, 1):
            if not s <= b < s + SPAN:
                continue
            allowed = key_ids == jnp.broadcast_to(ids_buf[4 + s, 0:1, :], (BLOCK, BLOCK))
            if b == 4 + s:
                allowed = allowed & below
            bias[s, b - s] = jnp.where(allowed, 0.0, NONE)


    def out_local(i, s, g):
        columns = pl.ds(pl.multiple_of(u * HALF + g * GROUP_WIDTH, GROUP_WIDTH), GROUP_WIDTH)
        return pltpu.make_async_copy(out_buf.at[i, s, g], (o_hbm, dq_hbm)[i].at[:, columns], out_sem.at[i, 0, g])

    def out_remote(i, s, g):
        columns = pl.ds(pl.multiple_of(u * HALF + g * GROUP_WIDTH, GROUP_WIDTH), GROUP_WIDTH)
        return pltpu.make_async_remote_copy(
            out_buf.at[i, s, g], (o_hbm, dq_hbm)[i].at[:, columns],
            out_sem.at[i, 1, g], out_recv.at[i, g], device_id=(c, other), device_id_type=MESH)

    def partial(i, g, step, t):
        return pltpu.make_async_remote_copy(
            part.at[i, g, 2 * (REACH - step) + t], got.at[i, g, step, u],
            part_send.at[i, g, step, t], part_recv.at[i, g, step, u], device_id=(c - step, t), device_id_type=MESH)

    def partial_chip(i, g):
        return pltpu.make_async_remote_copy(
            part.at[i, g, 4 + other], got.at[i, g, 0, u],
            part_send.at[i, g, 0, 0], part_recv.at[i, g, 0, 0], device_id=(c, other), device_id_type=MESH)

    def pairs(g, s):
        for pair in range(GROUP // 2):
            heads = [slice((2 * pair + h) * HEAD, (2 * pair + h + 1) * HEAD) for h in (0, 1)]
            yield pair, heads, [jnp.concatenate([buf[s, g, :, h] for h in heads], axis=0) for buf in (q_buf, g_buf)]

    def first(g, s):
        keys = kv_buf[0, g, pl.ds(s, SPAN)].reshape(ROWS, HEAD)
        add = bias[s].reshape(ROWS, BLOCK)
        add = jnp.concatenate([add, add], axis=1)
        dv = jnp.zeros((ROWS, HEAD), f32)
        for pair, heads, (qs, gs) in pairs(g, s):
            scores = dot(keys, qs, 1, 1) * TO_EXP2 + add
            probs = jnp.exp2(scores - jnp.max(scores, axis=0, keepdims=True))
            probs = (probs * (1.0 / jnp.sum(probs, axis=0, keepdims=True))).astype(bf16)
            probs_buf[g, s, pair] = probs
            dv = dv + dot(probs, gs, 1, 0)
        acc[1, pl.ds(s, SPAN)] += dv.reshape(SPAN, BLOCK, HEAD)

    def second(g, s):
        vals = kv_buf[1, g, pl.ds(s, SPAN)].reshape(ROWS, HEAD)
        dk = jnp.zeros((ROWS, HEAD), f32)
        for pair, heads, (qs, gs) in pairs(g, s):
            probs = probs_buf[g, s, pair].astype(f32)
            dprobs = dot(vals, gs, 1, 1)
            delta = jnp.sum(probs * dprobs, axis=0, keepdims=True)
            dscores = (probs * (dprobs - delta)).astype(bf16)
            dscores_buf[g, s, pair] = dscores
            dk = dk + dot(dscores, qs, 1, 0)
        acc[0, pl.ds(s, SPAN)] += dk.reshape(SPAN, BLOCK, HEAD) * SCALE

    def third(g, s):
        keys_t = jnp.transpose(kv_buf[0, g, pl.ds(s, SPAN)].reshape(ROWS, HEAD))
        vals_t = jnp.transpose(kv_buf[1, g, pl.ds(s, SPAN)].reshape(ROWS, HEAD))
        for pair in range(GROUP // 2):
            out_t = dot(vals_t, probs_buf[g, s, pair], 1, 0)
            dq_t = dot(keys_t, dscores_buf[g, s, pair], 1, 0) * SCALE
            for h in (0, 1):
                head = slice((2 * pair + h) * HEAD, (2 * pair + h + 1) * HEAD)
                out_buf[0, s, g, :, head] = jnp.transpose(out_t[:, h * BLOCK:(h + 1) * BLOCK]).astype(bf16)
                out_buf[1, s, g, :, head] = jnp.transpose(dq_t[:, h * BLOCK:(h + 1) * BLOCK]).astype(bf16)

    def send_partials(i, g):
        part[i, g] = acc[i].astype(bf16)
        def to(step, when):
            @pl.when(when & (c >= step))
            def _():
                for t in (0, 1):
                    partial(i, g, step, t).start()

        to(1, first_x)
        to(2, c >= 0)
        to(1, ~first_x)
        partial_chip(i, g).start()
        grad_buf[i, g, u] = acc[i, 4 + u]

    def head(g, carry):
        for i in range(2):
            own_q(i, g).wait()
            own_kv(i, g).wait()
        swap_kv(0, g).wait_recv()
        for i in range(2):
            swap_q(i, g).wait_recv()
        acc[...] = jnp.zeros(acc.shape, f32)
        halo_here(0, g)
        first(g, other)
        first(g, u)
        send_partials(1, g)

        swap_kv(1, g).wait_recv()
        halo_here(1, g)
        second(g, other)
        second(g, u)
        send_partials(0, g)
        return carry

    def rest(g, carry):
        third(g, other)
        for i in range(2):
            out_remote(i, other, g).start()
        third(g, u)
        for i in range(2):
            out_local(i, u, g).start()
        return carry

    def arrived(i, g, step, t):
        return pltpu.make_async_remote_copy(
            stage.at[i, g, 0], kv_buf.at[i, g, 2 * (REACH - step) + t],
            kv_send.at[i, g, step, t], kv_recv.at[i, g, step, t], device_id=(c, other), device_id_type=MESH)

    def later(i, g, step, t):
        return pltpu.make_async_remote_copy(
            part.at[i, g, 0], got.at[i, g, step, t], part_send.at[i, g, step, t],
            part_recv.at[i, g, step, t], device_id=(c, other), device_id_type=MESH)

    lax.fori_loop(0, LOCAL, head, 0)
    lax.fori_loop(0, LOCAL, rest, 0)

    for g in range(LOCAL):
        for i in (1, 0):
            partial_chip(i, g).wait_recv()
            grad_buf[i, g, other] = got[i, g, 0, other].astype(f32)
            for step in (1, 2):
                @pl.when(c + step < chips)
                def _():
                    for t in (0, 1):
                        later(i, g, step, t).wait_recv()
                        grad_buf[i, g, t] += got[i, g, step, t].astype(f32)
            for t in (0, 1):
                (dk_ref, dv_ref)[i][:, (t * LOCAL + g) * HEAD:(t * LOCAL + g + 1) * HEAD] = grad_buf[i, g, t].astype(bf16)

    for i in range(2):
        for g in range(LOCAL):
            halo_left(i, g)
    for g in range(LOCAL):
        for i in range(2):
            out_remote(i, other, g).wait()
            out_local(i, u, g).wait()
            swap_kv(i, g).wait_send()
            swap_q(i, g).wait_send()
            partial_chip(i, g).wait_send()
        for step in (1, 2):
            @pl.when(c >= step)
            def _():
                for i in range(2):
                    for t in (0, 1):
                        partial(i, g, step, t).wait_send()


def deliver(a0, a1, a2, a3, b0, b1, b2, b3, sem):
    copies = [pltpu.make_async_copy(a, b, sem.at[i]) for i, (a, b) in enumerate(zip((a0, a1, a2, a3), (b0, b1, b2, b3)))]
    for copy in copies:
        copy.start()
    for copy in copies:
        copy.wait()


def solution(mesh):
    chips = mesh.shape["ctx"]
    tokens = P(("ctx", "uly"), None)

    def per_device(queries, keys, values, output_gradient, segment_ids):
        rows = queries.shape[0]
        wide = jax.ShapeDtypeStruct((rows, 2 * HALF), bf16)
        narrow = jax.ShapeDtypeStruct((rows, 2 * LOCAL * HEAD), bf16)
        anywhere = pl.BlockSpec(memory_space=pltpu.HBM)
        vmem = pl.BlockSpec(memory_space=pltpu.VMEM)
        dma = pltpu.SemaphoreType.DMA
        held = pl.pallas_call(
            functools.partial(kernel, chips),
            out_shape=tuple(pltpu.VMEM(x.shape, x.dtype) for x in (wide, wide, narrow, narrow)),
            in_specs=[anywhere] * 5,
            out_specs=(vmem,) * 4,
            scratch_shapes=[
                pltpu.VMEM((2, LOCAL, BLOCK, GROUP_WIDTH), bf16),
                pltpu.VMEM((2, LOCAL, BLOCK, GROUP_WIDTH), bf16),
                pltpu.VMEM((2, LOCAL, 6, BLOCK, HEAD), bf16),
                pltpu.VMEM((6, 8, BLOCK), jnp.int32),
                pltpu.VMEM((2, SPAN, BLOCK, BLOCK), f32),
                pltpu.VMEM((2, 6, BLOCK, HEAD), f32),
                pltpu.VMEM((2, 2, LOCAL, BLOCK, GROUP_WIDTH), bf16),
                pltpu.VMEM((2, LOCAL, 6, BLOCK, HEAD), bf16),
                pltpu.VMEM((2, LOCAL, 3, 2, BLOCK, HEAD), bf16),
                pltpu.VMEM((2, LOCAL, 2, BLOCK, HEAD), f32),
                pltpu.VMEM((2, LOCAL, 2, BLOCK, HEAD), bf16),
                pltpu.VMEM((LOCAL, 2, GROUP // 2, ROWS, 2 * BLOCK), bf16),
                pltpu.VMEM((LOCAL, 2, GROUP // 2, ROWS, 2 * BLOCK), bf16),
                dma((LOCAL, 4)),
                dma((2, LOCAL, 2)),
                dma((6,)),
                dma((2, LOCAL)),
                dma((2, LOCAL)),
                dma((2, LOCAL, 3, 2)),
                dma((2, LOCAL, 3, 2)),
                dma((2, 2, LOCAL)),
                dma((2, LOCAL)),
                dma((2, LOCAL, 3, 2)),
                dma((2, LOCAL, 3, 2)),
            ],
            compiler_params=pltpu.CompilerParams(
                collective_id=0, has_side_effects=True, vmem_limit_bytes=48 * 2 ** 20),
        )(*[pltpu.with_memory_space_constraint(x, pltpu.HBM) for x in (
            queries, keys, values, output_gradient, segment_ids.reshape(-1, BLOCK))])
        return pl.pallas_call(
            deliver, out_shape=(wide, wide, narrow, narrow), in_specs=[vmem] * 4, out_specs=(anywhere,) * 4,
            scratch_shapes=[dma((4,))], compiler_params=pltpu.CompilerParams(vmem_limit_bytes=2 ** 20))(
                *[pltpu.with_memory_space_constraint(x, pltpu.VMEM) for x in held])

    return jax.shard_map(
        per_device, mesh=mesh, in_specs=(tokens,) * 4 + (P(),), out_specs=(tokens,) * 4, check_vma=False)
```

```python
import functools
import math

import jax
import jax.numpy as jnp
from jax import lax
from jax.experimental import pallas as pl
from jax.experimental.pallas import tpu as pltpu
from jax.sharding import PartitionSpec as P

MESH = pl.DeviceIdType.MESH
HEAD = 128
BLOCK = 128
GROUP = 4
GROUP_WIDTH = GROUP * HEAD
LOCAL = 2
HALF = LOCAL * GROUP_WIDTH
REACH = 2
RING = 4
SPAN = 5
ROWS = SPAN * BLOCK
SCALE = HEAD ** -0.5
TO_EXP2 = SCALE * math.log2(math.e)
NONE = -1e30

f32 = jnp.float32
bf16 = jnp.bfloat16


def dot(a, b, ca, cb):
    return lax.dot_general(a, b, (((ca,), (cb,)), ((), ())), preferred_element_type=f32)


def kernel(chips, q_hbm, k_hbm, v_hbm, g_hbm, ids_hbm, o_hbm, dq_hbm, dk_ref, dv_ref,
           q_buf, g_buf, kv_buf, ids_buf, bias, acc, out_buf, part, got, grad_buf, stage, probs_buf, dscores_buf,
           own_sem, stage_sem, ids_sem, qs_send, qs_recv, kv_send, kv_recv, out_sem, out_recv, part_send, part_recv):
    c, u = lax.axis_index("ctx"), lax.axis_index("uly")
    other = 1 - u
    kv_hbm = (k_hbm, v_hbm)
    odd = lax.rem(c, 2) == 1
    first_x = lax.rem(c, RING) == 0

    barrier = pltpu.get_barrier_semaphore()
    pl.semaphore_signal(barrier, inc=1, device_id=(c, other), device_id_type=MESH)
    for step in (1, 2):
        for t in (0, 1):
            @pl.when(c >= step)
            def _():
                pl.semaphore_signal(barrier, inc=1, device_id=(c - step, t), device_id_type=MESH)

    def own_q(i, g):
        columns = pl.ds(pl.multiple_of(u * HALF + g * GROUP_WIDTH, GROUP_WIDTH), GROUP_WIDTH)
        return pltpu.make_async_copy((q_hbm, g_hbm)[i].at[:, columns], (q_buf, g_buf)[i].at[u, g], own_sem.at[g, i])

    def own_kv(i, g):
        narrow = pl.ds(pl.multiple_of((u * LOCAL + g) * HEAD, HEAD), HEAD)
        return pltpu.make_async_copy(kv_hbm[i].at[:, narrow], kv_buf.at[i, g, 4 + u], own_sem.at[g, 2 + i])

    def staged(i, g, t):
        return pltpu.make_async_copy(
            kv_hbm[i].at[:, pl.ds((t * LOCAL + g) * HEAD, HEAD)], stage.at[i, g, t], stage_sem.at[i, g, t])

    ids_copies = []
    for b in range(6):
        row = jnp.maximum(2 * c - 4 + b, 0)
        ids_copies.append(pltpu.make_async_copy(ids_hbm.at[pl.ds(row, 1)], ids_buf.at[b, pl.ds(0, 1)], ids_sem.at[b]))
    for g in range(LOCAL):
        for i in range(2):
            for t in (0, 1):
                staged(i, g, t).start()
    for copy in ids_copies:
        copy.start()
    for g in range(LOCAL):
        for i in range(2):
            own_kv(i, g).start()
            own_q(i, g).start()

    for step in (1, 2):
        for i in range(2):
            @pl.when(c < step)
            def _():
                for g in range(LOCAL):
                    for t in (0, 1):
                        kv_buf[i, g, 2 * (REACH - step) + t] = jnp.zeros((BLOCK, HEAD), bf16)

    heard = 1
    for step in (1, 2):
        heard = heard + 2 * jnp.where(c + step < chips, 1, 0)
    for g in range(LOCAL):
        for i in range(2):
            for t in (0, 1):
                staged(i, g, t).wait()
    pl.semaphore_wait(barrier, heard)

    def halo(i, g, step, t):
        return pltpu.make_async_remote_copy(
            stage.at[i, g, t], kv_buf.at[i, g, 2 * (REACH - step) + u],
            kv_send.at[i, g, step, t], kv_recv.at[i, g, step, u], device_id=(c + step, t), device_id_type=MESH)

    def swap_kv(i, g):
        return pltpu.make_async_remote_copy(
            stage.at[i, g, other], kv_buf.at[i, g, 4 + u],
            kv_send.at[i, g, 0, 0], kv_recv.at[i, g, 0, 0], device_id=(c, other), device_id_type=MESH)

    def swap_q(i, g):
        columns = pl.ds(pl.multiple_of(other * HALF + g * GROUP_WIDTH, GROUP_WIDTH), GROUP_WIDTH)
        return pltpu.make_async_remote_copy(
            (q_hbm, g_hbm)[i].at[:, columns], (q_buf, g_buf)[i].at[u, g],
            qs_send.at[i, g], qs_recv.at[i, g], device_id=(c, other), device_id_type=MESH)

    def send_halo(i, g):
        def to(step, when):
            @pl.when(when & (c + step < chips))
            def _():
                for t in (0, 1):
                    halo(i, g, step, t).start()

        to(1, odd)
        to(2, c >= 0)
        to(1, ~odd)

    def halo_left(i, g):
        for step in (2, 1):
            @pl.when(c + step < chips)
            def _():
                for t in (0, 1):
                    halo(i, g, step, t).wait_send()

    def halo_here(i, g):
        for step in (1, 2):
            @pl.when(c >= step)
            def _():
                for t in (0, 1):
                    arrived(i, g, step, t).wait_recv()

    for g in range(LOCAL):
        for i in range(2):
            send_halo(i, g)
    for g in range(LOCAL):
        swap_kv(0, g).start()
        for i in range(2):
            swap_q(i, g).start()
        swap_kv(1, g).start()

    for copy in ids_copies:
        copy.wait()
    below = lax.broadcasted_iota(jnp.int32, (BLOCK, BLOCK), 0) <= lax.broadcasted_iota(jnp.int32, (BLOCK, BLOCK), 1)
    for b in range(6):
        key_ids = jnp.transpose(jnp.broadcast_to(ids_buf[b, 0:1, :], (BLOCK, BLOCK)))
        if b < 4:
            key_ids = jnp.where(c >= REACH - b // 2, key_ids, -1)
        for s in (0, 1):
            if not s <= b < s + SPAN:
                continue
            allowed = key_ids == jnp.broadcast_to(ids_buf[4 + s, 0:1, :], (BLOCK, BLOCK))
            if b == 4 + s:
                allowed = allowed & below
            bias[s, b - s] = jnp.where(allowed, 0.0, NONE)


    def out_local(i, s, g):
        columns = pl.ds(pl.multiple_of(u * HALF + g * GROUP_WIDTH, GROUP_WIDTH), GROUP_WIDTH)
        return pltpu.make_async_copy(out_buf.at[i, s, g], (o_hbm, dq_hbm)[i].at[:, columns], out_sem.at[i, 0, g])

    def out_remote(i, s, g):
        columns = pl.ds(pl.multiple_of(u * HALF + g * GROUP_WIDTH, GROUP_WIDTH), GROUP_WIDTH)
        return pltpu.make_async_remote_copy(
            out_buf.at[i, s, g], (o_hbm, dq_hbm)[i].at[:, columns],
            out_sem.at[i, 1, g], out_recv.at[i, g], device_id=(c, other), device_id_type=MESH)

    def partial(i, g, step, t):
        return pltpu.make_async_remote_copy(
            part.at[i, g, 2 * (REACH - step) + t], got.at[i, g, step, u],
            part_send.at[i, g, step, t], part_recv.at[i, g, step, u], device_id=(c - step, t), device_id_type=MESH)

    def partial_chip(i, g):
        return pltpu.make_async_remote_copy(
            part.at[i, g, 4 + other], got.at[i, g, 0, u],
            part_send.at[i, g, 0, 0], part_recv.at[i, g, 0, 0], device_id=(c, other), device_id_type=MESH)

    def pairs(g, s):
        for pair in range(GROUP // 2):
            heads = [slice((2 * pair + h) * HEAD, (2 * pair + h + 1) * HEAD) for h in (0, 1)]
            yield pair, heads, [jnp.concatenate([buf[s, g, :, h] for h in heads], axis=0) for buf in (q_buf, g_buf)]

    def first(g, s):
        keys = kv_buf[0, g, pl.ds(s, SPAN)].reshape(ROWS, HEAD)
        add = bias[s].reshape(ROWS, BLOCK)
        add = jnp.concatenate([add, add], axis=1)
        dv = jnp.zeros((ROWS, HEAD), f32)
        for pair, heads, (qs, gs) in pairs(g, s):
            scores = dot(keys, qs, 1, 1) * TO_EXP2 + add
            probs = jnp.exp2(scores - jnp.max(scores, axis=0, keepdims=True))
            probs = (probs * (1.0 / jnp.sum(probs, axis=0, keepdims=True))).astype(bf16)
            probs_buf[g, s, pair] = probs
            dv = dv + dot(probs, gs, 1, 0)
        acc[1, pl.ds(s, SPAN)] += dv.reshape(SPAN, BLOCK, HEAD)

    def second(g, s):
        vals = kv_buf[1, g, pl.ds(s, SPAN)].reshape(ROWS, HEAD)
        dk = jnp.zeros((ROWS, HEAD), f32)
        for pair, heads, (qs, gs) in pairs(g, s):
            probs = probs_buf[g, s, pair].astype(f32)
            dprobs = dot(vals, gs, 1, 1)
            delta = jnp.sum(probs * dprobs, axis=0, keepdims=True)
            dscores = (probs * (dprobs - delta)).astype(bf16)
            dscores_buf[g, s, pair] = dscores
            dk = dk + dot(dscores, qs, 1, 0)
        acc[0, pl.ds(s, SPAN)] += dk.reshape(SPAN, BLOCK, HEAD) * SCALE

    def third(g, s):
        keys_t = jnp.transpose(kv_buf[0, g, pl.ds(s, SPAN)].reshape(ROWS, HEAD))
        vals_t = jnp.transpose(kv_buf[1, g, pl.ds(s, SPAN)].reshape(ROWS, HEAD))
        for pair in range(GROUP // 2):
            out_t = dot(vals_t, probs_buf[g, s, pair], 1, 0)
            dq_t = dot(keys_t, dscores_buf[g, s, pair], 1, 0) * SCALE
            for h in (0, 1):
                head = slice((2 * pair + h) * HEAD, (2 * pair + h + 1) * HEAD)
                out_buf[0, s, g, :, head] = jnp.transpose(out_t[:, h * BLOCK:(h + 1) * BLOCK]).astype(bf16)
                out_buf[1, s, g, :, head] = jnp.transpose(dq_t[:, h * BLOCK:(h + 1) * BLOCK]).astype(bf16)

    def send_partials(i, g):
        part[i, g, 0:4] = acc[i, 0:4].astype(bf16)
        def to(step, when):
            @pl.when(when & (c >= step))
            def _():
                for t in (0, 1):
                    partial(i, g, step, t).start()

        to(1, first_x)
        to(2, c >= 0)
        to(1, ~first_x)
        part[i, g, 4:6] = acc[i, 4:6].astype(bf16)
        partial_chip(i, g).start()
        grad_buf[i, g, u] = acc[i, 4 + u]

    def head(g, carry):
        for i in range(2):
            own_q(i, g).wait()
            own_kv(i, g).wait()
        swap_kv(0, g).wait_recv()
        for i in range(2):
            swap_q(i, g).wait_recv()
        acc[...] = jnp.zeros(acc.shape, f32)
        halo_here(0, g)
        first(g, other)
        first(g, u)
        send_partials(1, g)

        swap_kv(1, g).wait_recv()
        halo_here(1, g)
        second(g, other)
        second(g, u)
        send_partials(0, g)
        return carry

    def rest(g, carry):
        third(g, other)
        for i in range(2):
            out_remote(i, other, g).start()
        third(g, u)
        for i in range(2):
            out_local(i, u, g).start()
        return carry

    def arrived(i, g, step, t):
        return pltpu.make_async_remote_copy(
            stage.at[i, g, 0], kv_buf.at[i, g, 2 * (REACH - step) + t],
            kv_send.at[i, g, step, t], kv_recv.at[i, g, step, t], device_id=(c, other), device_id_type=MESH)

    def later(i, g, step, t):
        return pltpu.make_async_remote_copy(
            part.at[i, g, 0], got.at[i, g, step, t], part_send.at[i, g, step, t],
            part_recv.at[i, g, step, t], device_id=(c, other), device_id_type=MESH)

    lax.fori_loop(0, LOCAL, head, 0)
    lax.fori_loop(0, LOCAL, rest, 0)

    def collect(i, g):
        partial_chip(i, g).wait_recv()
        grad_buf[i, g, other] = got[i, g, 0, other].astype(f32)
        for step in (1, 2):
            @pl.when(c + step < chips)
            def _():
                for t in (0, 1):
                    later(i, g, step, t).wait_recv()
                    grad_buf[i, g, t] += got[i, g, step, t].astype(f32)
        for t in (0, 1):
            (dk_ref, dv_ref)[i][:, (t * LOCAL + g) * HEAD:(t * LOCAL + g + 1) * HEAD] = grad_buf[i, g, t].astype(bf16)

    def partials_left(i, g):
        partial_chip(i, g).wait_send()
        for step in (1, 2):
            @pl.when(c >= step)
            def _():
                for t in (0, 1):
                    partial(i, g, step, t).wait_send()

    for g in range(LOCAL):
        for i in range(2):
            halo_left(i, g)
            swap_kv(i, g).wait_send()
            swap_q(i, g).wait_send()
    for g in range(LOCAL):
        for i in range(2):
            out_remote(i, other, g).wait()
            out_local(i, u, g).wait()
    for i, g in ((1, 0), (0, 0), (1, 1), (0, 1)):
        partials_left(i, g)
        collect(i, g)


def deliver(a0, a1, a2, a3, b0, b1, b2, b3, sem):
    copies = [pltpu.make_async_copy(a, b, sem.at[i]) for i, (a, b) in enumerate(zip((a0, a1, a2, a3), (b0, b1, b2, b3)))]
    for copy in copies:
        copy.start()
    for copy in copies:
        copy.wait()


def solution(mesh):
    chips = mesh.shape["ctx"]
    tokens = P(("ctx", "uly"), None)

    def per_device(queries, keys, values, output_gradient, segment_ids):
        rows = queries.shape[0]
        wide = jax.ShapeDtypeStruct((rows, 2 * HALF), bf16)
        narrow = jax.ShapeDtypeStruct((rows, 2 * LOCAL * HEAD), bf16)
        anywhere = pl.BlockSpec(memory_space=pltpu.HBM)
        vmem = pl.BlockSpec(memory_space=pltpu.VMEM)
        dma = pltpu.SemaphoreType.DMA
        held = pl.pallas_call(
            functools.partial(kernel, chips),
            out_shape=tuple(pltpu.VMEM(x.shape, x.dtype) for x in (wide, wide, narrow, narrow)),
            in_specs=[anywhere] * 5,
            out_specs=(vmem,) * 4,
            scratch_shapes=[
                pltpu.VMEM((2, LOCAL, BLOCK, GROUP_WIDTH), bf16),
                pltpu.VMEM((2, LOCAL, BLOCK, GROUP_WIDTH), bf16),
                pltpu.VMEM((2, LOCAL, 6, BLOCK, HEAD), bf16),
                pltpu.VMEM((6, 8, BLOCK), jnp.int32),
                pltpu.VMEM((2, SPAN, BLOCK, BLOCK), f32),
                pltpu.VMEM((2, 6, BLOCK, HEAD), f32),
                pltpu.VMEM((2, 2, LOCAL, BLOCK, GROUP_WIDTH), bf16),
                pltpu.VMEM((2, LOCAL, 6, BLOCK, HEAD), bf16),
                pltpu.VMEM((2, LOCAL, 3, 2, BLOCK, HEAD), bf16),
                pltpu.VMEM((2, LOCAL, 2, BLOCK, HEAD), f32),
                pltpu.VMEM((2, LOCAL, 2, BLOCK, HEAD), bf16),
                pltpu.VMEM((LOCAL, 2, GROUP // 2, ROWS, 2 * BLOCK), bf16),
                pltpu.VMEM((LOCAL, 2, GROUP // 2, ROWS, 2 * BLOCK), bf16),
                dma((LOCAL, 4)),
                dma((2, LOCAL, 2)),
                dma((6,)),
                dma((2, LOCAL)),
                dma((2, LOCAL)),
                dma((2, LOCAL, 3, 2)),
                dma((2, LOCAL, 3, 2)),
                dma((2, 2, LOCAL)),
                dma((2, LOCAL)),
                dma((2, LOCAL, 3, 2)),
                dma((2, LOCAL, 3, 2)),
            ],
            compiler_params=pltpu.CompilerParams(
                collective_id=0, has_side_effects=True, vmem_limit_bytes=48 * 2 ** 20),
        )(*[pltpu.with_memory_space_constraint(x, pltpu.HBM) for x in (
            queries, keys, values, output_gradient, segment_ids.reshape(-1, BLOCK))])
        return pl.pallas_call(
            deliver, out_shape=(wide, wide, narrow, narrow), in_specs=[vmem] * 4, out_specs=(anywhere,) * 4,
            scratch_shapes=[dma((4,))], compiler_params=pltpu.CompilerParams(vmem_limit_bytes=2 ** 20))(
                *[pltpu.with_memory_space_constraint(x, pltpu.VMEM) for x in held])

    return jax.shard_map(
        per_device, mesh=mesh, in_specs=(tokens,) * 4 + (P(),), out_specs=(tokens,) * 4, check_vma=False)
```
